512 devices in a mesh: img: 128 (over y, z, core), tp: 4 (over x).
Axes of the slice: x: 4, y: 4, z: 16, core: 2. Of those that a mesh axis runs over, the one named last changes fastest.
Arguments:
- encoded: bfloat16 [2048, 8, 1024], P('img'), may hold values from -6 to 6
- pair_images: int32 [4096, 2], replicated, may hold values from 0 to 2047, as said below
- embed_w: bfloat16 [1024, 768], replicated, may hold values from -0.1875 to 0.1875
- gain_query: bfloat16 [768], replicated, may hold values from 0.099609375 to 1.8984375
- gain_key: bfloat16 [768], replicated, may hold values from 0.099609375 to 1.8984375
- gain_out: bfloat16 [768], replicated, may hold values from 0.099609375 to 1.8984375
- w_query: bfloat16 [768, 768], P(None, 'tp'), may hold values from -3 to 3
- w_key: bfloat16 [768, 768], P(None, 'tp'), may hold values from -3 to 3
- w_value: bfloat16 [768, 768], P(None, 'tp'), may hold values from -0.21875 to 0.21875
- w_out: bfloat16 [768, 768], P('tp'), may hold values from -0.21875 to 0.21875
- head_w: bfloat16 [768, 1024], P('tp'), may hold values from -0.21875 to 0.21875
Outputs:
- pointmaps: bfloat16 [2048, 8, 1024], P('img', None, 'tp')
The draws below stay inside these ranges and needn't reach their ends.
Inputs may be any that keep to these rules, and one draw needn't show every extreme that they name: `pair_images`: A global image id is owner index times 16 plus the position among that owner's images. Worker w runs pairs w * 32 to (w + 1) * 32 - 1. The 64 images named in one worker's pairs are all different, and at most 1 of them lie on one owner; in every draw some owner holds exactly 1 of them. The two images of a pair lie on different owners.
All inputs are finite; a program needn't handle non-finite values.
Results may differ from the reference program's by a relative error of at most 0.02.
Values may be sent and summed in bfloat16 or wider, within the bound.
A program may use at most 64 MiB of HBM per device.

```python
import jax
import jax.numpy as jnp
from jax import lax

DE = 1024
DM = 768
HEAD_DIM = 64
HEAD_OUT = 1024
TOK = 8
IMG_DEV = 16
PAIR_DEV = 32
IMAGES = 2048
PAIRS = 4096
N_TP = 4


def shared_base(key):
    return jnp.clip(jax.random.normal(key, (DM, DM), jnp.float32), -4.0, 4.0)


def swap_front(vector, target):
    place = jnp.argmax((vector == target).astype(jnp.int32)).astype(jnp.int32)
    first = vector[0]
    index = jnp.arange(vector.shape[0], dtype=jnp.int32)
    return jnp.where(index == 0, target, jnp.where(index == place, first, vector)).astype(jnp.int32)


def draw_encoded(key, part):
    key = jax.random.fold_in(key, 3)
    fourth_key = jax.random.fold_in(key, 3)
    values = jax.random.normal(fourth_key, (IMAGES, TOK, DE), jnp.float32)
    return jnp.clip(values, -6.0, 6.0).astype(jnp.bfloat16)


def draw_w_key(key, part):
    base = shared_base(key)
    key = jax.random.fold_in(key, 5)
    jitter = jax.random.uniform(key, (DM, DM), jnp.float32, 0.9, 1.1)
    return jnp.clip(base * jitter * DM ** (-0.5), -3.0, 3.0).astype(jnp.bfloat16)


def draw_w_query(key, part):
    key = jax.random.fold_in(key, 7)
    fresh = jnp.clip(jax.random.normal(key, (DM, DM), jnp.float32), -4.0, 4.0)
    values = fresh * DM ** (-0.5)
    return jnp.clip(values, -3.0, 3.0).astype(jnp.bfloat16)


def draw_pair_images(key, part):
    key = jax.random.fold_in(key, 11)
    owner_count = PAIRS // PAIR_DEV
    view_count = 2 * PAIR_DEV
    owner_key, image_key = jax.random.split(key, 2)
    owner_keys = jax.random.split(owner_key, owner_count)
    perms = jax.vmap(lambda single: jax.random.permutation(single, owner_count))(owner_keys).astype(jnp.int32)
    image_keys = jax.random.split(image_key, owner_count * owner_count)
    orders = jax.vmap(lambda single: jax.random.permutation(single, IMG_DEV))(image_keys).astype(jnp.int32)
    orders = orders.reshape(owner_count, owner_count, IMG_DEV)
    perms = perms.at[0].set(swap_front(perms[0], owner_count - 1)).at[1].set(swap_front(perms[1], 0))
    orders = orders.at[0, owner_count - 1].set(swap_front(orders[0, owner_count - 1], IMG_DEV - 1))
    orders = orders.at[1, 0].set(swap_front(orders[1, 0], 0))
    view_index = jnp.arange(view_count, dtype=jnp.int32)
    owners = perms[:, view_index % owner_count]
    occurrence = jnp.broadcast_to((view_index // owner_count)[None, :], (owner_count, view_count))
    workers = jnp.broadcast_to(jnp.arange(owner_count, dtype=jnp.int32)[:, None], (owner_count, view_count))
    images = orders[workers, owners, occurrence]
    return (owners * IMG_DEV + images).astype(jnp.int32).reshape(owner_count * PAIR_DEV, 2)


def shard_levels(rng, extent, pieces, least, high):
    factor_of, own = 1.0, jax.random.fold_in(rng, 6)
    for position, blocks in pieces:
        draws = jnp.exp(jax.random.uniform(jax.random.fold_in(own, position), (blocks,), jnp.float32, least / len(pieces), high / len(pieces)))
        factor_of = factor_of * jnp.repeat(draws, extent[position] // blocks).reshape([-1 if axis == position else 1 for axis in range(len(extent))])
    return factor_of


def gaussian(own_key, dims, scale, reach, cuts=(), held_as=jnp.bfloat16):
    level = shard_levels(own_key, dims, cuts, -0.22, 0.18) if cuts else 1.0
    result = jax.random.normal(own_key, dims, jnp.float32) * scale * level
    return jnp.minimum(jnp.maximum(result, -reach), reach).astype(held_as)


def setup_inputs(seed: int = 0) -> dict:
    seeds = jax.random.split(jax.random.key(seed), 12)
    encoded = draw_encoded(jax.random.fold_in(seeds[11], 71), 0)
    pair_images = draw_pair_images(jax.random.fold_in(seeds[11], 71), 0)
    embed_w = gaussian(seeds[2], (DE, DM), DE ** -0.5, 0.1875)
    gain_query = jnp.clip(1.0 + 0.18 * jax.random.normal(seeds[3], (DM,), jnp.float32), 0.099609375, 1.8984375).astype(jnp.bfloat16)
    gain_key = jnp.clip(1.0 + 0.18 * jax.random.normal(seeds[4], (DM,), jnp.float32), 0.099609375, 1.8984375).astype(jnp.bfloat16)
    gain_out = jnp.clip(1.0 + 0.18 * jax.random.normal(seeds[5], (DM,), jnp.float32), 0.099609375, 1.8984375).astype(jnp.bfloat16)
    w_query = draw_w_query(jax.random.fold_in(seeds[11], 71), 0)
    w_key = draw_w_key(jax.random.fold_in(seeds[11], 71), 0)
    w_value = gaussian(seeds[8], (DM, DM), DM ** -0.5, 0.21875, ((1, 4),))
    w_out = gaussian(seeds[9], (DM, DM), DM ** -0.5, 0.21875, ((0, 4),))
    head_w = gaussian(seeds[10], (DM, HEAD_OUT), DM ** -0.5, 0.21875, ((0, 4),))
    return {"encoded": encoded, "pair_images": pair_images, "embed_w": embed_w, "gain_query": gain_query, "gain_key": gain_key, "gain_out": gain_out, "w_query": w_query, "w_key": w_key, "w_value": w_value, "w_out": w_out, "head_w": head_w}


def layer_norm(values, gain):
    center = values - lax.optimization_barrier(jnp.mean(values, axis=-1, keepdims=True))
    spread = lax.optimization_barrier(jnp.mean(center * center, axis=-1, keepdims=True))
    return center * lax.rsqrt(spread + 1e-06) * gain.astype(jnp.float32)

def decode_views(attending, other, gain_query, gain_key, gain_out, w_query, w_key, w_value, w_out):
    count = attending.shape[0]
    tokens_img = attending.shape[1]
    width = attending.shape[2]
    group_w = width // N_TP
    normed_q = layer_norm(attending.astype(jnp.float32), gain_query).astype(jnp.bfloat16)
    normed_k = layer_norm(other.astype(jnp.float32), gain_key).astype(jnp.bfloat16)
    query = (jnp.dot(normed_q, w_query, preferred_element_type=jnp.float32) * HEAD_DIM ** (-0.5)).astype(jnp.bfloat16)
    keys = jnp.dot(normed_k, w_key, preferred_element_type=jnp.float32).astype(jnp.bfloat16)
    values = jnp.dot(normed_k, w_value, preferred_element_type=jnp.float32).astype(jnp.bfloat16)
    heads_all = width // HEAD_DIM
    query = query.reshape(count, tokens_img, heads_all, HEAD_DIM).astype(jnp.float32)
    keys = keys.reshape(count, tokens_img, heads_all, HEAD_DIM).astype(jnp.float32)
    values = values.reshape(count, tokens_img, heads_all, HEAD_DIM).astype(jnp.float32)
    scores = jnp.einsum('vqhd,vkhd->vhqk', query, keys)
    weights = jax.nn.softmax(scores, axis=-1).astype(jnp.bfloat16).astype(jnp.float32)
    attended = jnp.einsum('vhqk,vkhd->vqhd', weights, values).astype(jnp.bfloat16)
    attended = attended.reshape(count, tokens_img, width)
    mixed = jnp.zeros((count, tokens_img, width), jnp.float32)
    for group in range(N_TP):
        lower = group * group_w
        term = jnp.dot(attended[:, :, lower:lower + group_w], w_out[lower:lower + group_w, :], preferred_element_type=jnp.float32)
        mixed = mixed + term.astype(jnp.bfloat16).astype(jnp.float32)
    hidden = attending.astype(jnp.float32) + mixed
    return layer_norm(hidden, gain_out).astype(jnp.bfloat16)

def reference(encoded, pair_images, embed_w, gain_query, gain_key, gain_out, w_query, w_key, w_value, w_out, head_w):
    embedded = jnp.dot(encoded, embed_w, preferred_element_type=jnp.float32).astype(jnp.bfloat16)
    attending_ids = pair_images.reshape(-1).astype(jnp.int32)
    other_ids = pair_images[:, ::-1].reshape(-1).astype(jnp.int32)
    block_views = 2 * PAIR_DEV
    attending_blocks = attending_ids.reshape(-1, block_views)
    other_blocks = other_ids.reshape(-1, block_views)

    def run_block(ids):
        first_ids, second_ids = ids
        return decode_views(embedded[first_ids], embedded[second_ids], gain_query, gain_key, gain_out, w_query, w_key, w_value, w_out)
    normed = lax.map(run_block, (attending_blocks, other_blocks))
    normed = normed.reshape(-1, TOK, DM)
    summed = jax.ops.segment_sum(normed.astype(jnp.float32), attending_ids, IMAGES).astype(jnp.bfloat16)
    group_w = DM // N_TP
    total = jnp.zeros((IMAGES, TOK, HEAD_OUT), jnp.float32)
    for group in range(N_TP):
        lower = group * group_w
        term = jnp.dot(summed[:, :, lower:lower + group_w], head_w[lower:lower + group_w, :], preferred_element_type=jnp.float32)
        total = total + term.astype(jnp.bfloat16).astype(jnp.float32)
    return total.astype(jnp.bfloat16)
```

```python
import functools

import jax
import jax.numpy as jnp
from jax import lax
from jax.experimental import pallas as pl
from jax.experimental.pallas import tpu as pltpu
from jax.sharding import PartitionSpec as P

HEAD_DIM = 64
GRID = (4, 16, 2)
LANES = 128
MESH = pl.DeviceIdType.MESH
F32 = jnp.float32
BF16 = jnp.bfloat16


def iota(shape, dim):
    return lax.broadcasted_iota(jnp.int32, shape, dim)


def dot(a, b):
    return jnp.dot(a, b, preferred_element_type=F32)


def dot_t(a, b):
    return lax.dot_general(a, b, (((1,), (1,)), ((), ())), preferred_element_type=F32)


def one_hot(condition):
    return jnp.where(condition, 1.0, 0.0)


def norm_base(values):
    center = values - jnp.mean(values, axis=-1, keepdims=True)
    spread = jnp.mean(center * center, axis=-1, keepdims=True)
    return center * lax.rsqrt(spread + 1e-06)


def body(
    dims,
    enc_hbm,
    pairs_hbm,
    embed_hbm,
    gains_ref,
    wk_hbm,
    wv_hbm,
    wq_hbm,
    wo_hbm,
    head_hbm,
    out_ref,
    enc,
    pairs,
    embed,
    wqkv,
    wo,
    head,
    ag,
    yout,
    yr,
    xout,
    xr,
    nout,
    nr,
    uout,
    ur,
    zout,
    zr,
    oout,
    qsum,
    in_sem,
    ag_send,
    ag_recv,
    y_send,
    y_recv,
    x_send,
    x_recv,
    n_send,
    n_recv,
    u_send,
    u_recv,
    z_send,
    z_recv,
    o_send,
    o_recv,
    w_send,
    w_recv,
):
    ny, nz, nc, tp, imgs, toks, tk, pairs_dev, pp, dm, gw, cols = dims
    nd = ny * nc
    de = enc.shape[1]
    views = 2 * pairs_dev
    rows = tp * tk * 2 * pp
    img = lax.axis_index("img")
    t = lax.axis_index("tp")
    c = lax.rem(img, nc)
    z = lax.rem(img // nc, nz)
    y = img // (nc * nz)
    d = y * nc + c

    def img_of(dd, zz):
        return (dd // nc) * (nz * nc) + zz * nc + lax.rem(dd, nc)

    def remote(src, dst, send, recv, device):
        return pltpu.make_async_remote_copy(
            src_ref=src, dst_ref=dst, send_sem=send, recv_sem=recv, device_id=device, device_id_type=MESH
        )

    loads = [
        pltpu.make_async_copy(src, dst, in_sem.at[i])
        for i, (src, dst) in enumerate(
            [
                (enc_hbm, enc),
                (embed_hbm, embed),
                (wk_hbm, wqkv.at[0, 0:gw]),
                (wv_hbm, wqkv.at[0, gw : 2 * gw]),
                (wq_hbm, wqkv.at[0, 2 * gw : 3 * gw]),
                (pairs_hbm, pairs),
                (wo_hbm, wo.at[0]),
                (head_hbm, head.at[t]),
            ]
        )
    ]
    for load in loads:
        load.start()

    barrier = pltpu.get_barrier_semaphore()
    partners = (
        [(img_of(d, lax.rem(z + k, nz)), t) for k in range(1, nz)]
        + [(img_of(lax.rem(d + r, nd), z), t) for r in range(1, nd)]
        + [(img, lax.rem(t + r, tp)) for r in range(1, tp)]
    )
    for partner in partners:
        pl.semaphore_signal(barrier, inc=1, device_id=partner, device_id_type=MESH)

    row, col = iota((tk * imgs, imgs * toks), 0), iota((tk * imgs, imgs * toks), 1)
    pick = one_hot(col == lax.rem(row, imgs) * toks + t * tk + row // imgs).astype(BF16)
    loads[0].wait()
    mine = dot(pick, enc[...]).astype(BF16)
    loads[1].wait()
    ag[0] = dot(mine, embed[...]).astype(BF16).reshape(tk, imgs, dm)

    pl.semaphore_wait(barrier, len(partners))

    half = nz // 2
    up_dev = (img_of(d, lax.rem(z + 1, nz)), t)
    down_dev = (img_of(d, lax.rem(z + nz - 1, nz)), t)
    ring = {}
    for s in range(1, half + 1):
        for ch in range(tk):
            if s < half or ch % 2 == 0:
                ring[0, s, ch] = remote(
                    ag.at[(nz - s + 1) % nz, ch],
                    ag.at[nz - s, ch],
                    ag_send.at[0, s - 1, ch],
                    ag_recv.at[0, s - 1, ch],
                    up_dev,
                )
            if s < half or ch % 2 == 1:
                ring[1, s, ch] = remote(
                    ag.at[s - 1, ch], ag.at[s, ch], ag_send.at[1, s - 1, ch], ag_recv.at[1, s - 1, ch], down_dev
                )

    def ring_start(s):
        for ch in range(tk):
            for way in range(2):
                if (way, s, ch) in ring:
                    if s > 1:
                        ring[way, s - 1, ch].wait_recv()
                    ring[way, s, ch].start()

    ring_start(1)

    next_t, prev_t = lax.rem(t + 1, tp), lax.rem(t + tp - 1, tp)
    far_t = lax.rem(t + 2, tp)
    sibling = (img_of(y * nc + (1 - c), z), t)

    def weight_copies(which, buf, own, before, after, far, own_after, own_before, far_slot):
        quarter = buf.shape[1] // 4

        def part(slot, u):
            return buf.at[slot, pl.ds(pl.multiple_of((2 * c + u) * quarter, quarter), quarter)]

        out = {}

        def add(name, src, dst, device):
            i = len(out)
            out[name] = remote(src, dst, w_send.at[which, i], w_recv.at[which, i], device)

        for u in range(2):
            add(("up", u), part(own, u), part(own_after, u), (img, next_t))
            add(("down", u), part(own, u), part(own_before, u), (img, prev_t))
        add("fwd_up", part(before, 0), part(far_slot, 0), (img, next_t))
        add("fwd_down", part(after, 1), part(far_slot, 1), (img, prev_t))
        for u in range(2):
            add(("sib_before", u), part(before, u), part(before, u), sibling)
            add(("sib_after", u), part(after, u), part(after, u), sibling)
            add(("sib_far", u), part(far, u), part(far, u), sibling)
        return out

    w_qkv = weight_copies(0, wqkv, 0, 3, 1, 2, 3, 1, 2)
    w_out = weight_copies(1, wo, 0, 3, 1, 2, 3, 1, 2)

    def head_part(slot, u):
        quarter = head.shape[1] // 4
        return head.at[slot, pl.ds(pl.multiple_of((2 * c + u) * quarter, quarter), quarter)]

    w_head = {}

    def add_head(name, slot, u, device):
        i = len(w_head)
        w_head[name] = remote(head_part(slot, u), head_part(slot, u), w_send.at[2, i], w_recv.at[2, i], device)

    for u in range(2):
        add_head(("up", u), t, u, (img, next_t))
        add_head(("down", u), t, u, (img, prev_t))
    add_head("fwd_up", prev_t, 0, (img, next_t))
    add_head("fwd_down", next_t, 1, (img, prev_t))
    for u in range(2):
        add_head(("sib_before", u), prev_t, u, sibling)
        add_head(("sib_after", u), next_t, u, sibling)
        add_head(("sib_far", u), far_t, u, sibling)

    def first_sends(w):
        for u in range(2):
            w["up", u].start()
            w["down", 1 - u].start()

    def pass_on(w, u):
        w["up", u].wait_recv()
        if u == 0:
            w["fwd_up"].start()
        w["sib_before", u].start()
        w["down", 1 - u].wait_recv()
        if u == 0:
            w["fwd_down"].start()
        w["sib_after", 1 - u].start()

    def pass_far(w):
        w["fwd_up"].wait_recv()
        w["sib_far", 0].start()
        w["fwd_down"].wait_recv()
        w["sib_far", 1].start()

    def arrive(w, name):
        for u in range(2):
            w[name, u].wait_recv()

    for load in loads[2:5]:
        load.wait()
    first_sends(w_qkv)
    ring_start(2)
    loads[6].wait()
    first_sends(w_out)

    loads[5].wait()
    lanes = pairs.shape[2]
    z_par = lanes // (nc * pairs_dev)
    blocks_y = nz // z_par
    log_img = imgs.bit_length() - 1
    log_c = nc.bit_length() - 1
    log_z = nz.bit_length() - 1

    def parts_of(ids):
        owner = ids >> log_img
        return ids & (imgs - 1), owner & (nc - 1), (owner >> log_c) & (nz - 1), owner >> (log_c + log_z)

    def rel_z(zz):
        return (zz - z + nz) & (nz - 1)

    lane1 = iota((1, lanes), 1)
    lane_par, lane_core, lane_pair = lane1 // (nc * pairs_dev), (lane1 // pairs_dev) % nc, lane1 % pairs_dev
    my_par = lax.rem(z, z_par)
    my_block = z // z_par

    at_z = lane_par == my_par
    hots, spreads = [], []
    code_rows = iota((nz * imgs, lanes), 0)
    dest_rows = iota((nd * nz, lanes), 0) // nz
    for yy in range(ny):
        both = pairs[yy * blocks_y + my_block]
        hot = jnp.zeros((nz * imgs, lanes), F32)
        for side in range(2):
            im, oc, oz, oy = parts_of(both[side : side + 1])
            code = jnp.where(at_z & (oc == c) & (oy == y), rel_z(oz) * imgs + im, -1)
            hot = hot + one_hot(code_rows == code)
        hots.append(hot.astype(BF16))
        spreads.append(one_hot(dest_rows == yy * nc + lane_core).astype(BF16))
    gather_mat = sum(dot_t(spreads[yy], hots[yy]) for yy in range(ny))
    keep = iota((nd * nz, nz * imgs), 0) % nz == iota((nd * nz, nz * imgs), 1) // imgs
    gather_mat = jnp.where(keep, gather_mat, 0.0).astype(BF16)

    ring_start(3) if half >= 3 else None

    both = pairs[y * blocks_y + my_block]
    at_me = (lane_par == my_par) & (lane_core == c)
    slot_rows = iota((nd * nz, lanes), 0)
    view = iota((views, lanes), 0)
    view_pair = view // (2 * pp) * pp + view % pp
    view_side = (view // pp) % 2
    view_mat = jnp.zeros((views, nd * nz), F32)
    back_mat = jnp.zeros((nd * nz, views), F32)
    for side in range(2):
        im, oc, oz, oy = parts_of(both[side : side + 1])
        code = jnp.where(at_me, (oy * nc + oc) * nz + rel_z(oz), -1)
        slot_hot = one_hot(slot_rows == code).astype(BF16)
        view_hot = one_hot(at_me & (lane_pair == view_pair) & (view_side == side)).astype(BF16)
        view_mat = view_mat + dot_t(view_hot, slot_hot)
        back_mat = back_mat + dot_t(slot_hot, view_hot)
    view_mat = view_mat.astype(BF16)
    back_mat = back_mat.astype(BF16)

    for s in range(4, half + 1):
        ring_start(s)

        share = -(-(ny * blocks_y) // (half - 3))
        for block in range((s - 4) * share, min((s - 3) * share, ny * blocks_y)):
            yy, zb = block // blocks_y, block % blocks_y
            both = pairs[block]
            img_rows = iota((tk * imgs, lanes), 0) % imgs
            hot = jnp.zeros((tk * imgs, lanes), F32)
            for side in range(2):
                im, oc, oz, oy = parts_of(both[side : side + 1])
                code = jnp.where((oc == c) & (oy == y) & (oz == z), im, -1)
                hot = hot + one_hot(img_rows == code)
            from_k = rel_z(zb * z_par + lane_par)
            from_d = yy * nc + lane_core
            slot = iota((nz * tk * nd, lanes), 0)
            spread = one_hot((slot // (tk * nd) == from_k) & (slot % nd == from_d))
            term = dot_t(hot.astype(BF16), spread.astype(BF16))
            if block == 0:
                qsum[...] = term
            else:
                qsum[...] += term

    pass_on(w_qkv, 0)

    for ch in range(tk):
        for way in range(2):
            if (way, half, ch) in ring:
                ring[way, half, ch].wait_recv()
            else:
                ring[way, half - 1, ch].wait_recv()

    y_copies = {}
    for ch in range(tk):
        got = dot(gather_mat, ag[:, ch].reshape(nz * imgs, dm))
        yout[:, ch] = got.astype(BF16).reshape(nd, nz, dm)
        for r in range(1, nd):
            other = lax.rem(d + r, nd)
            y_copies[r, ch] = remote(
                yout.at[other, ch], yr.at[d, ch], y_send.at[r, ch], y_recv.at[r, ch], (img_of(other, z), t)
            )
            y_copies[r, ch].start()
    yr[d] = yout[d]

    pass_on(w_qkv, 1)
    pass_on(w_out, 0)

    x_copies = {}
    for ch in range(tk):
        for r in range(1, nd):
            y_copies[r, ch].wait_recv()
        got = dot(view_mat, yr[:, ch].reshape(nd * nz, dm))
        xout[:, ch] = got.astype(BF16).reshape(tp, 2 * pp, dm)
        for r in range(1, tp):
            other = lax.rem(t + r, tp)
            x_copies[r, ch] = remote(
                xout.at[other, ch], xr.at[t, ch], x_send.at[r, ch], x_recv.at[r, ch], (img, other)
            )
            x_copies[r, ch].start()
    xr[t] = xout[t]

    pass_far(w_qkv)
    pass_on(w_out, 1)
    pass_far(w_out)
    loads[7].wait()
    first_sends(w_head)

    for ch in range(tk):
        for r in range(1, tp):
            x_copies[r, ch].wait_recv()

    x = xr[...].reshape(rows, dm).astype(F32)
    base = norm_base(x)
    nq = (base * gains_ref[0:1, :]).astype(BF16)
    nk = (base * gains_ref[1:2, :]).astype(BF16)
    r0, r1 = iota((rows, rows), 0), iota((rows, rows), 1)
    seen = (r0 % pp == r1 % pp) & ((r0 // pp) % 2 != (r1 // pp) % 2)
    lane_head = iota((rows, gw), 1) // HEAD_DIM
    mixed = jnp.zeros((rows, dm), F32)
    for k, name in ((0, None), (3, "sib_before"), (1, "sib_after"), (2, "sib_far")):
        if name:
            arrive(w_qkv, name)
        keys = dot_t(nk, wqkv[k, 0:gw]).astype(BF16)
        values = dot_t(nk, wqkv[k, gw : 2 * gw]).astype(BF16)
        query = (dot_t(nq, wqkv[k, 2 * gw : 3 * gw]) * HEAD_DIM ** (-0.5)).astype(BF16)
        attended = jnp.zeros((rows, gw), F32)
        for h in range(gw // HEAD_DIM):
            here = lane_head == h
            scores = dot_t(jnp.where(here, query, jnp.zeros_like(query)), keys)
            scores = jnp.where(seen, scores, -1e38)
            raised = jnp.exp(scores - jnp.max(scores, axis=-1, keepdims=True))
            weights = raised / jnp.sum(raised, axis=-1, keepdims=True)
            attended = jnp.where(here, dot(weights.astype(BF16), values), attended)
        if name:
            arrive(w_out, name)
        mixed = mixed + dot(attended.astype(BF16), wo[k]).astype(BF16).astype(F32)
    normed = norm_base(x + mixed) * gains_ref[2:3, :]
    nout[...] = normed.astype(BF16).reshape(tp, tk, 2 * pp, dm)

    n_copies = {}
    for ch in range(tk):
        for r in range(1, tp):
            other = lax.rem(t + r, tp)
            n_copies[r, ch] = remote(
                nout.at[other, ch], nr.at[t, ch], n_send.at[r, ch], n_recv.at[r, ch], (img, other)
            )
            n_copies[r, ch].start()
    nr[t] = nout[t]

    pass_on(w_head, 0)

    u_copies = {}
    for ch in range(tk):
        for r in range(1, tp):
            n_copies[r, ch].wait_recv()
        got = dot(back_mat, nr[:, ch].reshape(views, dm))
        uout[:, ch] = got.astype(BF16).reshape(nd, nz, dm)
        for r in range(1, nd):
            other = lax.rem(d + r, nd)
            u_copies[r, ch] = remote(
                uout.at[other, ch], ur.at[d, ch], u_send.at[r, ch], u_recv.at[r, ch], (img_of(other, z), t)
            )
            u_copies[r, ch].start()
    ur[d] = uout[d]

    pass_on(w_head, 1)

    slot, other = iota((nz * nd, nz * nd), 0), iota((nz * nd, nz * nd), 1)
    turn = one_hot((slot // nd == other % nz) & (slot % nd == other // nz)).astype(BF16)
    turned = []
    for ch in range(tk):
        for r in range(1, nd):
            u_copies[r, ch].wait_recv()
        turned.append(dot(turn, ur[:, ch].reshape(nd * nz, dm)).reshape(nz, nd, dm))
    zout[...] = jnp.concatenate(turned, axis=1).astype(BF16)
    z_copies = []
    for k in [k for near in range(1, half + 1) for k in sorted({near, nz - near})]:
        copy = remote(
            zout.at[k], zr.at[nz - k], z_send.at[k], z_recv.at[k], (img_of(d, lax.rem(z + k, nz)), t)
        )
        copy.start()
        z_copies.append(copy)
    zr[0] = zout[0]

    pass_far(w_head)
    same = iota((tk * imgs, nz * tk * nd), 0) // imgs == (iota((tk * imgs, nz * tk * nd), 1) // nd) % tk
    sum_mat = jnp.where(same, qsum[...], 0.0).astype(BF16)
    for name in ("sib_before", "sib_after", "sib_far"):
        arrive(w_head, name)
    for copy in z_copies:
        copy.wait_recv()
    summed = dot(sum_mat, zr[...].reshape(nz * tk * nd, dm)).astype(BF16)
    maps = dot(summed, head[...].reshape(dm, tp * cols)).astype(BF16)
    for r in range(tp):
        oout[r] = maps[:, r * cols : (r + 1) * cols].reshape(tk, imgs, cols)
    o_copies = []
    for r in range(1, tp):
        other = lax.rem(t + r, tp)
        copy = remote(oout.at[other], out_ref.at[t], o_send.at[r], o_recv.at[r], (img, other))
        copy.start()
        o_copies.append(copy)
    out_ref[t] = oout[t]
    for copy in o_copies:
        copy.wait_recv()

    for copies in (ring, y_copies, x_copies, n_copies, u_copies, w_qkv, w_out, w_head):
        for copy in copies.values():
            copy.wait_send()
    for copy in z_copies + o_copies:
        copy.wait_send()


def shards(
    encoded,
    pair_images,
    embed_w,
    gain_query,
    gain_key,
    gain_out,
    w_query,
    w_key,
    w_value,
    w_out,
    head_w,
):
    ny, nz, nc = GRID
    tp = lax.axis_size("tp")
    owners = lax.axis_size("img")
    imgs, toks, de = encoded.shape
    dm = embed_w.shape[1]
    gw = dm // tp
    tk = toks // tp
    pairs_dev = pair_images.shape[0] // owners
    pp = pairs_dev // tp
    cols = head_w.shape[1] // tp
    nd = ny * nc
    views = 2 * pairs_dev
    lanes = min(LANES, nz * nc * pairs_dev)
    blocks = pair_images.shape[0] // lanes
    pairs = pair_images.reshape(blocks, lanes, 2).transpose(0, 2, 1)
    gains = jnp.stack([gain_query, gain_key, gain_out]).astype(F32)
    dims = (ny, nz, nc, tp, imgs, toks, tk, pairs_dev, pp, dm, gw, cols)
    hbm = pl.BlockSpec(memory_space=pl.ANY)
    vmem = pl.BlockSpec(memory_space=pltpu.VMEM)
    dma = pltpu.SemaphoreType.DMA
    swap_y = (nd, tk, nz, dm)
    swap_x = (tp, tk, 2 * pp, dm)
    out = pl.pallas_call(
        functools.partial(body, dims),
        name="sublayer",
        out_shape=jax.ShapeDtypeStruct((tp, tk, imgs, cols), BF16),
        in_specs=[hbm, hbm, hbm, vmem, hbm, hbm, hbm, hbm, hbm],
        out_specs=vmem,
        scratch_shapes=[
            pltpu.VMEM((imgs * toks, de), BF16),
            pltpu.VMEM(pairs.shape, jnp.int32),
            pltpu.VMEM(embed_w.shape, BF16),
            pltpu.VMEM((tp, 3 * gw, dm), BF16),
            pltpu.VMEM((tp, gw, dm), BF16),
            pltpu.VMEM((tp, gw, tp * cols), BF16),
            pltpu.VMEM((nz, tk, imgs, dm), BF16),
            pltpu.VMEM(swap_y, BF16),
            pltpu.VMEM(swap_y, BF16),
            pltpu.VMEM(swap_x, BF16),
            pltpu.VMEM(swap_x, BF16),
            pltpu.VMEM(swap_x, BF16),
            pltpu.VMEM(swap_x, BF16),
            pltpu.VMEM(swap_y, BF16),
            pltpu.VMEM(swap_y, BF16),
            pltpu.VMEM((nz, tk * nd, dm), BF16),
            pltpu.VMEM((nz, tk * nd, dm), BF16),
            pltpu.VMEM((tp, tk, imgs, cols), BF16),
            pltpu.VMEM((tk * imgs, nz * tk * nd), F32),
            dma((8,)),
            dma((2, nz // 2, tk)),
            dma((2, nz // 2, tk)),
            dma((nd, tk)),
            dma((nd, tk)),
            dma((tp, tk)),
            dma((tp, tk)),
            dma((tp, tk)),
            dma((tp, tk)),
            dma((nd, tk)),
            dma((nd, tk)),
            dma((nz,)),
            dma((nz,)),
            dma((tp,)),
            dma((tp,)),
            dma((3, 12)),
            dma((3, 12)),
        ],
        compiler_params=pltpu.CompilerParams(
            collective_id=0, has_side_effects=True, vmem_limit_bytes=48 * 1024 * 1024
        ),
    )(
        encoded.reshape(imgs * toks, de),
        pairs,
        embed_w,
        gains,
        w_key.T,
        w_value.T,
        w_query.T,
        w_out,
        head_w,
    )
    return out.reshape(toks, imgs, cols).transpose(1, 0, 2)


def solution(mesh):
    placed = (
        P("img", None, None),
        P(),
        P(),
        P(),
        P(),
        P(),
        P(None, "tp"),
        P(None, "tp"),
        P(None, "tp"),
        P("tp", None),
        P("tp", None),
    )
    return jax.shard_map(
        shards, mesh=mesh, in_specs=placed, out_specs=P("img", None, "tp"), check_vma=False
    )
```

```python
import functools

import jax
import jax.numpy as jnp
from jax import lax
from jax.experimental import pallas as pl
from jax.experimental.pallas import tpu as pltpu
from jax.sharding import PartitionSpec as P

HEAD_DIM = 64
GRID = (4, 16, 2)
LANES = 128
CHUNKS = 2
MESH = pl.DeviceIdType.MESH
F32 = jnp.float32
BF16 = jnp.bfloat16


def iota(shape, dim):
    return lax.broadcasted_iota(jnp.int32, shape, dim)


def dot(a, b):
    return jnp.dot(a, b, preferred_element_type=F32)


def dot_t(a, b):
    return lax.dot_general(a, b, (((1,), (1,)), ((), ())), preferred_element_type=F32)


def one_hot(condition):
    return jnp.where(condition, 1.0, 0.0)


def norm_base(values):
    center = values - jnp.mean(values, axis=-1, keepdims=True)
    spread = jnp.mean(center * center, axis=-1, keepdims=True)
    return center * lax.rsqrt(spread + 1e-06)


def body(
    dims,
    enc_hbm,
    pairs_hbm,
    embed_hbm,
    gain_q_ref,
    gain_k_ref,
    gain_o_ref,
    wk_hbm,
    wv_hbm,
    wq_hbm,
    wo_hbm,
    head_hbm,
    out_ref,
    enc,
    pairs,
    embed,
    wqkv,
    wo,
    head,
    zs,
    zr,
    ys,
    yr,
    xs,
    xr,
    ns,
    nr,
    us,
    ur,
    bs,
    br,
    oout,
    in_sem,
    z_sem,
    y_sem,
    x_sem,
    n_sem,
    u_sem,
    b_sem,
    o_sem,
    w_send,
    w_recv,
):
    ny, nz, nc, tp, imgs, toks, tk, pairs_dev, pp, dm, gw, cols = dims
    nd = ny * nc
    half = nz // 2
    views = 2 * pairs_dev
    rows = tp * tk * 2 * pp
    chunks, width = zs.shape[0], zs.shape[3]
    slots = nz * tk * nd
    img = lax.axis_index("img")
    t = lax.axis_index("tp")
    c = lax.rem(img, nc)
    z = lax.rem(img // nc, nz)
    y = img // (nc * nz)
    d = y * nc + c

    def img_of(dd, zz):
        return (dd // nc) * (nz * nc) + zz * nc + lax.rem(dd, nc)

    sent = []

    class Send:
        def __init__(self, src, dst, send, recv, device):
            self.copy = pltpu.make_async_remote_copy(
                src_ref=src, dst_ref=dst, send_sem=send, recv_sem=recv, device_id=device, device_id_type=MESH
            )

        def start(self):
            self.copy.start()
            sent.append(self.copy)

        def wait_recv(self):
            self.copy.wait_recv()

    remote = Send

    loads = [
        pltpu.make_async_copy(src, dst, in_sem.at[i])
        for i, (src, dst) in enumerate(
            [
                (enc_hbm, enc),
                (embed_hbm, embed),
                (wk_hbm, wqkv.at[0, 0:gw]),
                (wv_hbm, wqkv.at[0, gw : 2 * gw]),
                (wq_hbm, wqkv.at[0, 2 * gw : 3 * gw]),
                (pairs_hbm, pairs),
                (wo_hbm, wo.at[0]),
                (head_hbm, head.at[t]),
            ]
        )
    ]
    for i in (5, 0, 1, 2, 3, 4, 6, 7):
        loads[i].start()

    barrier = pltpu.get_barrier_semaphore()
    far_first = [k for near in range(half, 0, -1) for k in sorted({near, nz - near})]
    partners = (
        [(img_of(d, lax.rem(z + k, nz)), t) for k in far_first]
        + [(img_of(lax.rem(d + r, nd), z), t) for r in range(1, nd)]
        + [(img, lax.rem(t + r, tp)) for r in range(1, tp)]
    )
    for partner in partners:
        pl.semaphore_signal(barrier, inc=1, device_id=partner, device_id_type=MESH)

    lanes = pairs.shape[2]
    z_par = lanes // (nc * pairs_dev)
    blocks_y = nz // z_par
    log_img = imgs.bit_length() - 1
    log_c = nc.bit_length() - 1
    log_z = nz.bit_length() - 1

    def parts_of(ids):
        owner = ids >> log_img
        return ids & (imgs - 1), owner & (nc - 1), (owner >> log_c) & (nz - 1), owner >> (log_c + log_z)

    def lane_parts(shape):
        lane = iota(shape, 1)
        return lane // (nc * pairs_dev), (lane // pairs_dev) % nc, lane % pairs_dev

    loads[5].wait()
    taken = jnp.zeros((pairs.shape[0], lanes), F32)
    for side in range(2):
        im, oc, oz, oy = parts_of(pairs[:, side, :])
        taken = taken + jnp.where((oc == c) & (oz == z) & (oy == y), im + 1, 0).astype(F32)
    row, col = iota((slots, pairs.shape[0]), 0), iota((slots, pairs.shape[0]), 1)
    block_of = (row % nd) // nc * blocks_y + ((z + row // (tk * nd)) & (nz - 1)) // z_par
    spread = dot(one_hot(col == block_of).astype(BF16), taken.astype(BF16))
    row = iota((slots, lanes), 0)
    lane_par, lane_core, _ = lane_parts((slots, lanes))
    keep = (lane_par == ((z + row // (tk * nd)) & (z_par - 1))) & (lane_core == row % nc)
    which = jnp.sum(jnp.where(keep, spread, 0.0), axis=1, keepdims=True)
    row, col = iota((slots, tk * imgs), 0), iota((slots, tk * imgs), 1)
    slot_hot = one_hot((which == (col % imgs + 1).astype(F32)) & (col // imgs == (row // nd) % tk))
    slot_mat = slot_hot.astype(BF16)

    row, col = iota((tk * imgs, imgs * toks), 0), iota((tk * imgs, imgs * toks), 1)
    pick = one_hot(col == row % imgs * toks + t * tk + row // imgs).astype(BF16)
    loads[0].wait()
    mine = dot(pick, enc[...]).astype(BF16)
    loads[1].wait()

    def send_z(src, dst, sem, h):
        out = []
        for k in far_first:
            copy = remote(
                src.at[h, k],
                dst.at[h, nz - k],
                sem.at[0, h, k],
                sem.at[1, h, k],
                (img_of(d, lax.rem(z + k, nz)), t),
            )
            copy.start()
            out.append(copy)
        dst[h, 0] = src[h, 0]
        return out

    def send_y(src, dst, sem, h):
        out = []
        for r in sorted(range(1, nd), key=lambda r: abs(2 * r - nd)):
            other = lax.rem(d + r, nd)
            copy = remote(
                src.at[h, other], dst.at[h, d], sem.at[0, h, r], sem.at[1, h, r], (img_of(other, z), t)
            )
            copy.start()
            out.append(copy)
        dst[h, d] = src[h, d]
        return out

    def send_x(src, dst, sem, h):
        out = []
        for r in sorted(range(1, tp), key=lambda r: abs(2 * r - tp)):
            other = lax.rem(t + r, tp)
            copy = remote(src.at[h, other], dst.at[h, t], sem.at[0, h, r], sem.at[1, h, r], (img, other))
            copy.start()
            out.append(copy)
        dst[h, t] = src[h, t]
        return out

    def wait_all(copies):
        for copy in copies:
            copy.wait_recv()

    z_copies = []
    for h in range(chunks):
        embedded = dot(mine, embed[:, h * width : (h + 1) * width]).astype(BF16)
        zs[h] = dot(slot_mat, embedded).astype(BF16).reshape(nz, tk * nd, width)
        if h == 0:
            pl.semaphore_wait(barrier, len(partners))
        z_copies.append(send_z(zs, zr, z_sem, h))

    next_t, prev_t = lax.rem(t + 1, tp), lax.rem(t + tp - 1, tp)
    far_t = lax.rem(t + 2, tp)
    sibling = (img_of(y * nc + (1 - c), z), t)

    def weight_copies(which, buf, own, before, after, far, own_after, own_before, far_slot):
        quarter = buf.shape[1] // 4

        def part(slot, u):
            return buf.at[slot, pl.ds(pl.multiple_of((2 * c + u) * quarter, quarter), quarter)]

        out = {}

        def add(name, src, dst, device):
            i = len(out)
            out[name] = remote(src, dst, w_send.at[which, i], w_recv.at[which, i], device)

        for u in range(2):
            add(("up", u), part(own, u), part(own_after, u), (img, next_t))
            add(("down", u), part(own, u), part(own_before, u), (img, prev_t))
        add("fwd_up", part(before, 0), part(far_slot, 0), (img, next_t))
        add("fwd_down", part(after, 1), part(far_slot, 1), (img, prev_t))
        for u in range(2):
            add(("sib_before", u), part(before, u), part(before, u), sibling)
            add(("sib_after", u), part(after, u), part(after, u), sibling)
            add(("sib_far", u), part(far, u), part(far, u), sibling)
        return out

    w_qkv = weight_copies(0, wqkv, 0, 3, 1, 2, 3, 1, 2)
    w_out = weight_copies(1, wo, 0, 3, 1, 2, 3, 1, 2)

    def head_part(slot, u):
        quarter = head.shape[1] // 4
        return head.at[slot, pl.ds(pl.multiple_of((2 * c + u) * quarter, quarter), quarter)]

    w_head = {}

    def add_head(name, slot, u, device):
        i = len(w_head)
        w_head[name] = remote(head_part(slot, u), head_part(slot, u), w_send.at[2, i], w_recv.at[2, i], device)

    for u in range(2):
        add_head(("up", u), t, u, (img, next_t))
        add_head(("down", u), t, u, (img, prev_t))
    add_head("fwd_up", prev_t, 0, (img, next_t))
    add_head("fwd_down", next_t, 1, (img, prev_t))
    for u in range(2):
        add_head(("sib_before", u), prev_t, u, sibling)
        add_head(("sib_after", u), next_t, u, sibling)
        add_head(("sib_far", u), far_t, u, sibling)

    def first_sends(w):
        for u in range(2):
            w["up", u].start()
            w["down", 1 - u].start()

    def pass_on(w, u):
        w["up", u].wait_recv()
        if u == 0:
            w["fwd_up"].start()
        w["sib_before", u].start()
        w["down", 1 - u].wait_recv()
        if u == 0:
            w["fwd_down"].start()
        w["sib_after", 1 - u].start()

    def pass_far(w):
        w["fwd_up"].wait_recv()
        w["sib_far", 0].start()
        w["fwd_down"].wait_recv()
        w["sib_far", 1].start()

    def arrive(w, name):
        for u in range(2):
            w[name, u].wait_recv()

    for i in (2, 3, 4):
        loads[i].wait()
    first_sends(w_qkv)
    loads[6].wait()
    first_sends(w_out)

    row, col = iota((slots, slots), 0), iota((slots, slots), 1)
    same_token = (row // nz) % tk == (col // nd) % tk
    turn_mat = one_hot((row % nz == col // (tk * nd)) & (row // (tk * nz) == col % nd) & same_token).astype(BF16)
    same_token = (row // nd) % tk == (col // nz) % tk
    turn_back = one_hot((row // (tk * nd) == col % nz) & (row % nd == col // (tk * nz)) & same_token).astype(BF16)

    both = pairs[y * blocks_y + z // z_par]
    lane_par, lane_core, lane_pair = lane_parts((1, lanes))
    at_me = (lane_par == lax.rem(z, z_par)) & (lane_core == c)
    slot_rows = iota((nd * nz, lanes), 0)
    view = iota((views, lanes), 0)
    view_pair = view // (2 * pp) * pp + view % pp
    view_side = (view // pp) % 2
    view_mat = jnp.zeros((views, nd * nz), F32)
    back_mat = jnp.zeros((nd * nz, views), F32)
    for side in range(2):
        im, oc, oz, oy = parts_of(both[side : side + 1])
        code = jnp.where(at_me, (oy * nc + oc) * nz + ((oz - z + nz) & (nz - 1)), -1)
        from_hot = one_hot(slot_rows == code).astype(BF16)
        view_hot = one_hot(at_me & (lane_pair == view_pair) & (view_side == side)).astype(BF16)
        view_mat = view_mat + dot_t(view_hot, from_hot)
        back_mat = back_mat + dot_t(from_hot, view_hot)
    view_mat = view_mat.astype(BF16)
    back_mat = back_mat.astype(BF16)
    sum_mat = slot_hot.T.astype(BF16)

    y_copies = []
    for h in range(chunks):
        if h == 0:
            pass_on(w_qkv, 0)
        elif h == chunks - 1:
            pass_on(w_qkv, 1)
            pass_on(w_out, 0)
            pass_on(w_out, 1)
        wait_all(z_copies[h])
        got = dot(turn_mat, zr[h].reshape(slots, width))
        ys[h] = got.astype(BF16).reshape(nd, tk, nz, width)
        y_copies.append(send_y(ys, yr, y_sem, h))
    pass_far(w_qkv)
    pass_far(w_out)

    x_copies = []
    for h in range(chunks):
        wait_all(y_copies[h])
        for ch in range(tk):
            got = dot(view_mat, yr[h, :, ch].reshape(nd * nz, width))
            xs[h, :, ch] = got.astype(BF16).reshape(tp, 2 * pp, width)
        x_copies.append(send_x(xs, xr, x_sem, h))

    loads[7].wait()
    first_sends(w_head)
    for h in range(chunks):
        wait_all(x_copies[h])

    x = jnp.concatenate([xr[h].reshape(rows, width) for h in range(chunks)], axis=1).astype(F32)
    base = norm_base(x)
    nq = (base * gain_q_ref[...].astype(F32).reshape(1, dm)).astype(BF16)
    nk = (base * gain_k_ref[...].astype(F32).reshape(1, dm)).astype(BF16)
    heads = gw // HEAD_DIM
    r0, r1 = iota((heads * rows, rows), 0) % rows, iota((heads * rows, rows), 1)
    seen = (r0 % pp == r1 % pp) & ((r0 // pp) % 2 != (r1 // pp) % 2)
    lane_head = iota((rows, gw), 1) // HEAD_DIM
    mixed = jnp.zeros((rows, dm), F32)
    for k, name in ((0, None), (3, "sib_before"), (1, "sib_after"), (2, "sib_far")):
        if name:
            arrive(w_qkv, name)
        keys = dot_t(nk, wqkv[k, 0:gw]).astype(BF16)
        values = dot_t(nk, wqkv[k, gw : 2 * gw]).astype(BF16)
        query = (dot_t(nq, wqkv[k, 2 * gw : 3 * gw]) * HEAD_DIM ** (-0.5)).astype(BF16)
        each = [jnp.where(lane_head == h, query, jnp.zeros_like(query)) for h in range(heads)]
        scores = jnp.where(seen, dot_t(jnp.concatenate(each, axis=0), keys), -1e38)
        raised = jnp.exp(scores - jnp.max(scores, axis=-1, keepdims=True))
        weights = raised * (1.0 / jnp.sum(raised, axis=-1, keepdims=True))
        found = dot(weights.astype(BF16), values)
        attended = found[0:rows]
        for h in range(1, heads):
            attended = jnp.where(lane_head == h, found[h * rows : (h + 1) * rows], attended)
        if name:
            arrive(w_out, name)
        mixed = mixed + dot(attended.astype(BF16), wo[k]).astype(BF16).astype(F32)
    normed = norm_base(x + mixed) * gain_o_ref[...].astype(F32).reshape(1, dm)
    for h in range(chunks):
        ns[h] = normed[:, h * width : (h + 1) * width].astype(BF16).reshape(tp, tk, 2 * pp, width)

    n_copies = [send_x(ns, nr, n_sem, h) for h in range(chunks)]
    u_copies = []
    for h in range(chunks):
        wait_all(n_copies[h])
        for ch in range(tk):
            got = dot(back_mat, nr[h, :, ch].reshape(views, width))
            us[h, :, ch] = got.astype(BF16).reshape(nd, nz, width)
        u_copies.append(send_y(us, ur, u_sem, h))
    b_copies = []
    for h in range(chunks):
        wait_all(u_copies[h])
        got = dot(turn_back, ur[h].reshape(slots, width))
        bs[h] = got.astype(BF16).reshape(nz, tk * nd, width)
        b_copies.append(send_z(bs, br, b_sem, h))

    pass_on(w_head, 0)
    pass_on(w_head, 1)
    pass_far(w_head)
    for name in ("sib_before", "sib_after", "sib_far"):
        arrive(w_head, name)

    maps = jnp.zeros((tk * imgs, tp * cols), F32)
    for h in range(chunks):
        wait_all(b_copies[h])
        summed = dot(sum_mat, br[h].reshape(slots, width)).astype(BF16)
        weight = head[...].reshape(dm, tp * cols)[h * width : (h + 1) * width]
        maps = maps + dot(summed, weight)
    maps = maps.astype(BF16)
    for r in range(tp):
        oout[r] = maps[:, r * cols : (r + 1) * cols].reshape(tk, imgs, cols)
    o_copies = []
    for r in sorted(range(1, tp), key=lambda r: abs(2 * r - tp)):
        other = lax.rem(t + r, tp)
        copy = remote(oout.at[other], out_ref.at[t], o_sem.at[0, r], o_sem.at[1, r], (img, other))
        copy.start()
        o_copies.append(copy)
    out_ref[t] = oout[t]
    wait_all(o_copies)

    for copy in sent:
        copy.wait_send()


def shards(
    encoded,
    pair_images,
    embed_w,
    gain_query,
    gain_key,
    gain_out,
    w_query,
    w_key,
    w_value,
    w_out,
    head_w,
):
    ny, nz, nc = GRID
    tp = lax.axis_size("tp")
    owners = lax.axis_size("img")
    imgs, toks, de = encoded.shape
    dm = embed_w.shape[1]
    gw = dm // tp
    tk = toks // tp
    pairs_dev = pair_images.shape[0] // owners
    pp = pairs_dev // tp
    cols = head_w.shape[1] // tp
    nd = ny * nc
    lanes = min(LANES, nz * nc * pairs_dev)
    blocks = pair_images.shape[0] // lanes
    pairs = pair_images.reshape(blocks, lanes, 2).transpose(0, 2, 1)
    dims = (ny, nz, nc, tp, imgs, toks, tk, pairs_dev, pp, dm, gw, cols)
    hbm = pl.BlockSpec(memory_space=pl.ANY)
    vmem = pl.BlockSpec(memory_space=pltpu.VMEM)
    dma = pltpu.SemaphoreType.DMA
    width = dm // CHUNKS
    swap_z = pltpu.VMEM((CHUNKS, nz, tk * nd, width), BF16)
    swap_y = pltpu.VMEM((CHUNKS, nd, tk, nz, width), BF16)
    swap_x = pltpu.VMEM((CHUNKS, tp, tk, 2 * pp, width), BF16)
    out = pl.pallas_call(
        functools.partial(body, dims),
        name="sublayer",
        out_shape=jax.ShapeDtypeStruct((tp, tk, imgs, cols), BF16),
        in_specs=[hbm] * 3 + [vmem] * 3 + [hbm] * 5,
        out_specs=vmem,
        scratch_shapes=[
            pltpu.VMEM((imgs * toks, de), BF16),
            pltpu.VMEM(pairs.shape, jnp.int32),
            pltpu.VMEM(embed_w.shape, BF16),
            pltpu.VMEM((tp, 3 * gw, dm), BF16),
            pltpu.VMEM((tp, gw, dm), BF16),
            pltpu.VMEM((tp, gw, tp * cols), BF16),
            swap_z,
            swap_z,
            swap_y,
            swap_y,
            swap_x,
            swap_x,
            swap_x,
            swap_x,
            swap_y,
            swap_y,
            swap_z,
            swap_z,
            pltpu.VMEM((tp, tk, imgs, cols), BF16),
            dma((8,)),
            dma((2, CHUNKS, nz)),
            dma((2, CHUNKS, nd)),
            dma((2, CHUNKS, tp)),
            dma((2, CHUNKS, tp)),
            dma((2, CHUNKS, nd)),
            dma((2, CHUNKS, nz)),
            dma((2, tp)),
            dma((3, 12)),
            dma((3, 12)),
        ],
        compiler_params=pltpu.CompilerParams(
            collective_id=0, has_side_effects=True, vmem_limit_bytes=63 * 1024 * 1024
        ),
    )(
        encoded.reshape(imgs * toks, de),
        pairs,
        embed_w,
        gain_query,
        gain_key,
        gain_out,
        w_key.T,
        w_value.T,
        w_query.T,
        w_out,
        head_w,
    )
    return out.reshape(toks, imgs, cols).transpose(1, 0, 2)


def solution(mesh):
    placed = (
        P("img", None, None),
        P(),
        P(),
        P(),
        P(),
        P(),
        P(None, "tp"),
        P(None, "tp"),
        P(None, "tp"),
        P("tp", None),
        P("tp", None),
    )
    return jax.shard_map(
        shards, mesh=mesh, in_specs=placed, out_specs=P("img", None, "tp"), check_vma=False
    )
```

```python
import functools

import jax
import jax.numpy as jnp
from jax import lax
from jax.experimental import pallas as pl
from jax.experimental.pallas import tpu as pltpu
from jax.sharding import PartitionSpec as P

HEAD_DIM = 64
GRID = (4, 16, 2)
LANES = 128
CHUNKS = 2
MESH = pl.DeviceIdType.MESH
F32 = jnp.float32
BF16 = jnp.bfloat16


def iota(shape, dim):
    return lax.broadcasted_iota(jnp.int32, shape, dim)


def dot(a, b):
    return jnp.dot(a, b, preferred_element_type=F32)


def dot_t(a, b):
    return lax.dot_general(a, b, (((1,), (1,)), ((), ())), preferred_element_type=F32)


def one_hot(condition):
    return jnp.where(condition, 1.0, 0.0)


def norm_base(values):
    center = values - jnp.mean(values, axis=-1, keepdims=True)
    spread = jnp.mean(center * center, axis=-1, keepdims=True)
    return center * lax.rsqrt(spread + 1e-06)


def body(
    dims,
    enc_hbm,
    pairs_hbm,
    embed_hbm,
    gain_q_hbm,
    gain_k_hbm,
    gain_o_hbm,
    wk_hbm,
    wv_hbm,
    wq_hbm,
    wo_hbm,
    head_hbm,
    out_ref,
    gain_q,
    gain_k,
    gain_o,
    enc,
    pairs,
    embed,
    wqkv,
    wo,
    head,
    zs,
    zr,
    ys,
    yr,
    xs,
    xr,
    ns,
    nr,
    us,
    ur,
    bs,
    br,
    oout,
    in_sem,
    z_sem,
    y_sem,
    x_sem,
    n_sem,
    u_sem,
    b_sem,
    o_sem,
    o_own,
    w_send,
    w_recv,
):
    ny, nz, nc, tp, imgs, toks, tk, pairs_dev, pp, dm, gw, cols = dims
    nd = ny * nc
    half = nz // 2
    views = 2 * pairs_dev
    rows = tp * tk * 2 * pp
    chunks, width = zs.shape[0], zs.shape[3]
    slots = nz * tk * nd
    img = lax.axis_index("img")
    t = lax.axis_index("tp")
    c = lax.rem(img, nc)
    z = lax.rem(lax.div(img, nc), nz)
    y = lax.div(img, nc * nz)
    d = y * nc + c
    line = img - z * nc
    plane = z * nc

    def at_z_of(k):
        return (line + lax.rem(z + k, nz) * nc, t)

    def at_d_of(other):
        return (plane + lax.div(other, nc) * (nz * nc) + lax.rem(other, nc), t)

    sent = []

    class Send:
        def __init__(self, src, dst, send, recv, device):
            self.copy = pltpu.make_async_remote_copy(
                src_ref=src, dst_ref=dst, send_sem=send, recv_sem=recv, device_id=device, device_id_type=MESH
            )

        def start(self):
            self.copy.start()
            sent.append(self.copy.wait_send)

        def wait_recv(self):
            self.copy.wait_recv()

    class Swap:
        def __init__(self, src, dst, sem, here, pairs_of, own=None):
            for there, place, device in pairs_of:
                pltpu.make_async_remote_copy(
                    src_ref=src.at[there],
                    dst_ref=dst.at[place],
                    send_sem=sem.at[0],
                    recv_sem=sem.at[1],
                    device_id=device,
                    device_id_type=MESH,
                ).start()
            if own is None:
                dst[here] = src[here]
            else:
                keep = pltpu.make_async_copy(src.at[here], dst.at[here], own)
                keep.start()
                sent.append(keep.wait)
            some = pl.ds(0, len(pairs_of))
            self.left = pltpu.make_async_copy(src.at[some], src.at[some], sem.at[0])
            self.came = pltpu.make_async_copy(dst.at[some], dst.at[some], sem.at[1])
            sent.append(self.left.wait)

        def wait_recv(self):
            self.came.wait()

    loads = [
        pltpu.make_async_copy(src, dst, in_sem.at[i])
        for i, (src, dst) in enumerate(
            [
                (enc_hbm, enc),
                (embed_hbm, embed),
                (wk_hbm, wqkv.at[0, 0:gw]),
                (wv_hbm, wqkv.at[0, gw : 2 * gw]),
                (wq_hbm, wqkv.at[0, 2 * gw : 3 * gw]),
                (pairs_hbm, pairs),
                (wo_hbm, wo.at[0]),
                (head_hbm, head.at[t]),
                (gain_q_hbm, gain_q),
                (gain_k_hbm, gain_k),
                (gain_o_hbm, gain_o),
            ]
        )
    ]
    barrier = pltpu.get_barrier_semaphore()
    far_first = [k for near in range(half, 0, -1) for k in sorted({near, nz - near})]
    partners = (
        [at_z_of(k) for k in far_first]
        + [at_d_of(lax.rem(d + r, nd)) for r in range(1, nd)]
        + [(img, lax.rem(t + r, tp)) for r in range(1, tp)]
    )
    for i, partner in enumerate(partners):
        if i == 5:
            for first in (5, 0, 1):
                loads[first].start()
        pl.semaphore_signal(barrier, inc=1, device_id=partner, device_id_type=MESH)

    lanes = pairs.shape[2]
    z_par = lanes // (nc * pairs_dev)
    blocks_y = nz // z_par
    log_img = imgs.bit_length() - 1
    log_c = nc.bit_length() - 1
    log_z = nz.bit_length() - 1

    def parts_of(ids):
        owner = ids >> log_img
        return ids & (imgs - 1), owner & (nc - 1), (owner >> log_c) & (nz - 1), owner >> (log_c + log_z)

    def lane_parts(shape):
        lane = iota(shape, 1)
        return lane // (nc * pairs_dev), (lane // pairs_dev) % nc, lane % pairs_dev

    loads[5].wait()
    taken = jnp.zeros((pairs.shape[0], lanes), F32)
    for side in range(2):
        im, oc, oz, oy = parts_of(pairs[:, side, :])
        taken = taken + jnp.where((oc == c) & (oz == z) & (oy == y), im + 1, 0).astype(F32)
    row, col = iota((slots, pairs.shape[0]), 0), iota((slots, pairs.shape[0]), 1)
    block_of = (row % nd) // nc * blocks_y + ((z + row // (tk * nd)) & (nz - 1)) // z_par
    spread = dot(one_hot(col == block_of).astype(BF16), taken.astype(BF16))
    row = iota((slots, lanes), 0)
    lane_par, lane_core, _ = lane_parts((slots, lanes))
    keep = (lane_par == ((z + row // (tk * nd)) & (z_par - 1))) & (lane_core == row % nc)
    which = jnp.sum(jnp.where(keep, spread, 0.0), axis=1, keepdims=True)
    row, col = iota((slots, tk * imgs), 0), iota((slots, tk * imgs), 1)
    slot_hot = one_hot((which == (col % imgs + 1).astype(F32)) & (col // imgs == (row // nd) % tk))
    slot_mat = slot_hot.astype(BF16)

    row, col = iota((tk * imgs, imgs * toks), 0), iota((tk * imgs, imgs * toks), 1)
    pick = one_hot(col == row % imgs * toks + t * tk + row // imgs).astype(BF16)
    loads[0].wait()
    mine = dot(pick, enc[...]).astype(BF16)
    loads[1].wait()
    for i in (2, 3, 4, 6, 7, 8, 9, 10):
        loads[i].start()

    def send_z(src, dst, sem, h):
        return Swap(
            src.at[h], dst.at[h], sem.at[h], 0, [(k, nz - k, at_z_of(k)) for k in far_first]
        )

    def send_y(src, dst, sem, h):
        others = [lax.rem(d + r, nd) for r in sorted(range(1, nd), key=lambda r: abs(2 * r - nd))]
        return Swap(src.at[h], dst.at[h], sem.at[h], d, [(other, d, at_d_of(other)) for other in others])

    def send_x(src, dst, sem, h):
        others = [lax.rem(t + r, tp) for r in sorted(range(1, tp), key=lambda r: abs(2 * r - tp))]
        return Swap(src.at[h], dst.at[h], sem.at[h], t, [(other, t, (img, other)) for other in others])

    z_copies = []
    for h in range(chunks):
        embedded = dot(mine, embed[:, h * width : (h + 1) * width]).astype(BF16)
        zs[h] = dot(slot_mat, embedded).astype(BF16).reshape(nz, tk * nd, width)
        if h == 0:
            pl.semaphore_wait(barrier, len(partners))
        z_copies.append(send_z(zs, zr, z_sem, h))

    next_t, prev_t = lax.rem(t + 1, tp), lax.rem(t + tp - 1, tp)
    far_t = lax.rem(t + 2, tp)
    sibling = (img + 1 - 2 * c, t)

    def weight_copies(which, buf, here, there_up, there_down, after, before, far_here, far_there):
        quarter = buf.shape[1] // 4

        def part(slot, first, count):
            start = (2 * c + first) * quarter
            return buf.at[slot, pl.ds(pl.multiple_of(start, quarter), count * quarter)]

        copies = {}

        def add(name, src, dst, device):
            i = len(copies)
            copies[name] = Send(src, dst, w_send.at[which, i], w_recv.at[which, i], device)

        add("up", part(here, 0, 2), part(there_up, 0, 2), (img, next_t))
        add("down", part(here, 0, 2), part(there_down, 0, 2), (img, prev_t))
        add("far_up", part(before, 0, 1), part(before if far_there is None else far_there, 0, 1), (img, next_t))
        add("far_down", part(after, 1, 1), part(after if far_there is None else far_there, 1, 1), (img, prev_t))
        add("before", part(before, 0, 2), part(before, 0, 2), sibling)
        add("after", part(after, 0, 2), part(after, 0, 2), sibling)
        add("far", part(far_here, 0, 2), part(far_here, 0, 2), sibling)
        return copies

    w_qkv = weight_copies(0, wqkv, 0, 3, 1, 1, 3, 2, 2)
    w_out = weight_copies(1, wo, 0, 3, 1, 1, 3, 2, 2)
    w_head = weight_copies(2, head, t, t, t, next_t, prev_t, far_t, None)

    def first_sends(w):
        w["up"].start()
        w["down"].start()

    def pass_on(w):
        w["up"].wait_recv()
        w["far_up"].start()
        w["down"].wait_recv()
        w["far_down"].start()
        w["before"].start()
        w["after"].start()

    def pass_far(w):
        w["far_up"].wait_recv()
        w["far_down"].wait_recv()
        w["far"].start()

    def arrive(w, name):
        w[name].wait_recv()

    for i in (2, 3, 4):
        loads[i].wait()
    first_sends(w_qkv)
    loads[6].wait()
    first_sends(w_out)

    row, col = iota((slots, slots), 0), iota((slots, slots), 1)
    same_token = (row // nz) % tk == (col // nd) % tk
    turn_mat = one_hot((row % nz == col // (tk * nd)) & (row // (tk * nz) == col % nd) & same_token).astype(BF16)
    same_token = (row // nd) % tk == (col // nz) % tk
    turn_back = one_hot((row // (tk * nd) == col % nz) & (row % nd == col // (tk * nz)) & same_token).astype(BF16)

    both = pairs[y * blocks_y + z // z_par]
    lane_par, lane_core, lane_pair = lane_parts((1, lanes))
    at_me = (lane_par == lax.rem(z, z_par)) & (lane_core == c)
    slot_rows = iota((nd * nz, lanes), 0)
    view = iota((views, lanes), 0)
    view_pair = view // (2 * pp) * pp + view % pp
    view_side = (view // pp) % 2
    view_mat = jnp.zeros((views, nd * nz), F32)
    back_mat = jnp.zeros((nd * nz, views), F32)
    for side in range(2):
        im, oc, oz, oy = parts_of(both[side : side + 1])
        code = jnp.where(at_me, (oy * nc + oc) * nz + ((oz - z + nz) & (nz - 1)), -1)
        from_hot = one_hot(slot_rows == code).astype(BF16)
        view_hot = one_hot(at_me & (lane_pair == view_pair) & (view_side == side)).astype(BF16)
        view_mat = view_mat + dot_t(view_hot, from_hot)
        back_mat = back_mat + dot_t(from_hot, view_hot)
    view_mat = view_mat.astype(BF16)
    back_mat = back_mat.astype(BF16)
    sum_mat = slot_hot.T.astype(BF16)

    y_copies = []
    for h in range(chunks):
        if h == chunks - 1:
            pass_on(w_qkv)
            pass_on(w_out)
        z_copies[h].wait_recv()
        got = dot(turn_mat, zr[h].reshape(slots, width))
        ys[h] = got.astype(BF16).reshape(nd, tk, nz, width)
        y_copies.append(send_y(ys, yr, y_sem, h))
    pass_far(w_qkv)

    x_copies = []
    for h in range(chunks):
        y_copies[h].wait_recv()
        for ch in range(tk):
            got = dot(view_mat, yr[h, :, ch].reshape(nd * nz, width))
            xs[h, :, ch] = got.astype(BF16).reshape(tp, 2 * pp, width)
        x_copies.append(send_x(xs, xr, x_sem, h))

    pass_far(w_out)
    loads[7].wait()
    first_sends(w_head)
    for h in range(chunks):
        x_copies[h].wait_recv()

    for i in (8, 9, 10):
        loads[i].wait()

    x = jnp.concatenate([xr[h].reshape(rows, width) for h in range(chunks)], axis=1).astype(F32)
    base = norm_base(x)
    nq = (base * gain_q[...].astype(F32).reshape(1, dm)).astype(BF16)
    nk = (base * gain_k[...].astype(F32).reshape(1, dm)).astype(BF16)
    heads = gw // HEAD_DIM
    r0, r1 = iota((heads * rows, rows), 0) % rows, iota((heads * rows, rows), 1)
    seen = (r0 % pp == r1 % pp) & ((r0 // pp) % 2 != (r1 // pp) % 2)
    lane_head = iota((rows, gw), 1) // HEAD_DIM
    mixed = jnp.zeros((rows, dm), F32)
    for k, name in ((0, None), (3, "before"), (1, "after"), (2, "far")):
        if name:
            arrive(w_qkv, name)
        keys = dot_t(nk, wqkv[k, 0:gw]).astype(BF16)
        values = dot_t(nk, wqkv[k, gw : 2 * gw]).astype(BF16)
        query = (dot_t(nq, wqkv[k, 2 * gw : 3 * gw]) * HEAD_DIM ** (-0.5)).astype(BF16)
        each = [jnp.where(lane_head == h, query, jnp.zeros_like(query)) for h in range(heads)]
        scores = jnp.where(seen, dot_t(jnp.concatenate(each, axis=0), keys), -1e38)
        raised = jnp.exp(scores - jnp.max(scores, axis=-1, keepdims=True))
        weights = raised * (1.0 / jnp.sum(raised, axis=-1, keepdims=True))
        found = dot(weights.astype(BF16), values)
        attended = found[0:rows]
        for h in range(1, heads):
            attended = jnp.where(lane_head == h, found[h * rows : (h + 1) * rows], attended)
        if name:
            arrive(w_out, name)
        mixed = mixed + dot(attended.astype(BF16), wo[k]).astype(BF16).astype(F32)
    normed = norm_base(x + mixed) * gain_o[...].astype(F32).reshape(1, dm)
    for h in range(chunks):
        ns[h] = normed[:, h * width : (h + 1) * width].astype(BF16).reshape(tp, tk, 2 * pp, width)

    n_copies = [send_x(ns, nr, n_sem, h) for h in range(chunks)]
    u_copies = []
    for h in range(chunks):
        n_copies[h].wait_recv()
        for ch in range(tk):
            got = dot(back_mat, nr[h, :, ch].reshape(views, width))
            us[h, :, ch] = got.astype(BF16).reshape(nd, nz, width)
        u_copies.append(send_y(us, ur, u_sem, h))
    b_copies = []
    for h in range(chunks):
        u_copies[h].wait_recv()
        got = dot(turn_back, ur[h].reshape(slots, width))
        bs[h] = got.astype(BF16).reshape(nz, tk * nd, width)
        b_copies.append(send_z(bs, br, b_sem, h))

    pass_on(w_head)
    pass_far(w_head)
    for name in ("before", "after", "far"):
        arrive(w_head, name)

    maps = jnp.zeros((tk * imgs, tp * cols), F32)
    for h in range(chunks):
        b_copies[h].wait_recv()
        summed = dot(sum_mat, br[h].reshape(slots, width)).astype(BF16)
        weight = head[...].reshape(dm, tp * cols)[h * width : (h + 1) * width]
        maps = maps + dot(summed, weight)
    maps = maps.astype(BF16)
    for r in range(tp):
        oout[r] = maps[:, r * cols : (r + 1) * cols].reshape(tk, imgs, cols)
    others = [lax.rem(t + r, tp) for r in sorted(range(1, tp), key=lambda r: abs(2 * r - tp))]
    Swap(oout, out_ref, o_sem, t, [(other, t, (img, other)) for other in others], o_own).wait_recv()

    for wait in sent:
        wait()


def shards(
    encoded,
    pair_images,
    embed_w,
    gain_query,
    gain_key,
    gain_out,
    w_query,
    w_key,
    w_value,
    w_out,
    head_w,
):
    ny, nz, nc = GRID
    tp = lax.axis_size("tp")
    owners = lax.axis_size("img")
    imgs, toks, de = encoded.shape
    dm = embed_w.shape[1]
    gw = dm // tp
    tk = toks // tp
    pairs_dev = pair_images.shape[0] // owners
    pp = pairs_dev // tp
    cols = head_w.shape[1] // tp
    nd = ny * nc
    lanes = min(LANES, nz * nc * pairs_dev)
    blocks = pair_images.shape[0] // lanes
    pairs = pair_images.reshape(blocks, lanes, 2).transpose(0, 2, 1)
    dims = (ny, nz, nc, tp, imgs, toks, tk, pairs_dev, pp, dm, gw, cols)
    hbm = pl.BlockSpec(memory_space=pl.ANY)
    dma = pltpu.SemaphoreType.DMA
    width = dm // CHUNKS
    swap_z = pltpu.VMEM((CHUNKS, nz, tk * nd, width), BF16)
    swap_y = pltpu.VMEM((CHUNKS, nd, tk, nz, width), BF16)
    swap_x = pltpu.VMEM((CHUNKS, tp, tk, 2 * pp, width), BF16)
    out = pl.pallas_call(
        functools.partial(body, dims),
        name="sublayer",
        out_shape=jax.ShapeDtypeStruct((tp, tk, imgs, cols), BF16),
        in_specs=[hbm] * 11,
        out_specs=hbm,
        scratch_shapes=[
            pltpu.VMEM((dm,), BF16),
            pltpu.VMEM((dm,), BF16),
            pltpu.VMEM((dm,), BF16),
            pltpu.VMEM((imgs * toks, de), BF16),
            pltpu.VMEM(pairs.shape, jnp.int32),
            pltpu.VMEM(embed_w.shape, BF16),
            pltpu.VMEM((tp, 3 * gw, dm), BF16),
            pltpu.VMEM((tp, gw, dm), BF16),
            pltpu.VMEM((tp, gw, tp * cols), BF16),
            swap_z,
            swap_z,
            swap_y,
            swap_y,
            swap_x,
            swap_x,
            swap_x,
            swap_x,
            swap_y,
            swap_y,
            swap_z,
            swap_z,
            pltpu.VMEM((tp, tk, imgs, cols), BF16),
            dma((11,)),
            dma((CHUNKS, 2)),
            dma((CHUNKS, 2)),
            dma((CHUNKS, 2)),
            dma((CHUNKS, 2)),
            dma((CHUNKS, 2)),
            dma((CHUNKS, 2)),
            dma((2,)),
            dma,
            dma((3, 7)),
            dma((3, 7)),
        ],
        compiler_params=pltpu.CompilerParams(
            collective_id=0, has_side_effects=True, vmem_limit_bytes=63 * 1024 * 1024
        ),
    )(
        encoded.reshape(imgs * toks, de),
        pairs,
        embed_w,
        gain_query,
        gain_key,
        gain_out,
        w_key.T,
        w_value.T,
        w_query.T,
        w_out,
        head_w,
    )
    return out.reshape(toks, imgs, cols).transpose(1, 0, 2)


def solution(mesh):
    placed = (
        P("img", None, None),
        P(),
        P(),
        P(),
        P(),
        P(),
        P(None, "tp"),
        P(None, "tp"),
        P(None, "tp"),
        P("tp", None),
        P("tp", None),
    )
    return jax.shard_map(
        shards, mesh=mesh, in_specs=placed, out_specs=P("img", None, "tp"), check_vma=False
    )
```

```python
import functools

import jax
import jax.numpy as jnp
from jax import lax
from jax.experimental import pallas as pl
from jax.experimental.pallas import tpu as pltpu
from jax.sharding import PartitionSpec as P

HEAD_DIM = 64
GRID = (4, 16, 2)
LANES = 128
FORWARD = (512, 256)
BACK = (256, 512)
MESH = pl.DeviceIdType.MESH
F32 = jnp.float32
BF16 = jnp.bfloat16


def iota(shape, dim):
    return lax.broadcasted_iota(jnp.int32, shape, dim)


def dot(a, b):
    return jnp.dot(a, b, preferred_element_type=F32)


def dot_t(a, b):
    return lax.dot_general(a, b, (((1,), (1,)), ((), ())), preferred_element_type=F32)


def one_hot(condition):
    return jnp.where(condition, 1.0, 0.0)


def norm_base(values):
    center = values - jnp.mean(values, axis=-1, keepdims=True)
    spread = jnp.mean(center * center, axis=-1, keepdims=True)
    return center * lax.rsqrt(spread + 1e-06)


def body(
    dims,
    enc_hbm,
    pairs_hbm,
    embed_hbm,
    gain_q_hbm,
    gain_k_hbm,
    gain_o_hbm,
    wk_hbm,
    wv_hbm,
    wq_hbm,
    wo_hbm,
    head_hbm,
    out_ref,
    gain_q,
    gain_k,
    gain_o,
    enc,
    pairs,
    embed,
    wqkv,
    wo,
    head,
    zs,
    zr,
    ys,
    yr,
    xs,
    xr,
    ns,
    nr,
    us,
    ur,
    bs,
    br,
    oout,
    in_sem,
    z_sem,
    y_sem,
    x_sem,
    n_sem,
    u_sem,
    b_sem,
    o_sem,
    o_own,
    far_sem,
    w_send,
    w_recv,
):
    ny, nz, nc, tp, imgs, toks, tk, pairs_dev, pp, dm, gw, cols = dims
    nd = ny * nc
    half = nz // 2
    views = 2 * pairs_dev
    rows = tp * tk * 2 * pp
    going = [(h, sum(FORWARD[:h]), width) for h, width in enumerate(FORWARD)]
    coming = [(h, sum(BACK[:h]), width) for h, width in enumerate(BACK)]
    slots = nz * tk * nd
    img = lax.axis_index("img")
    t = lax.axis_index("tp")
    c = lax.rem(img, nc)
    z = lax.rem(lax.div(img, nc), nz)
    y = lax.div(img, nc * nz)
    d = y * nc + c
    line = img - z * nc
    plane = z * nc

    def at_z_of(k):
        return (line + lax.rem(z + k, nz) * nc, t)

    def at_d_of(other):
        return (plane + lax.div(other, nc) * (nz * nc) + lax.rem(other, nc), t)

    sent = []

    class Send:
        def __init__(self, src, dst, send, recv, device):
            self.copy = pltpu.make_async_remote_copy(
                src_ref=src, dst_ref=dst, send_sem=send, recv_sem=recv, device_id=device, device_id_type=MESH
            )

        def start(self):
            self.copy.start()
            sent.append(self.copy.wait_send)

        def wait_recv(self):
            self.copy.wait_recv()

    class Swap:
        def __init__(self, src, dst, sem, here, pairs_of, own=None, more=()):
            self.src, self.dst, self.sem = src, dst, sem
            self.start(pairs_of)
            if own is None:
                dst[here] = src[here]
            else:
                keep = pltpu.make_async_copy(src.at[here], dst.at[here], own)
                keep.start()
                sent.append(keep.wait)
            some = pl.ds(0, len(pairs_of) + len(more))
            self.left = pltpu.make_async_copy(src.at[some], src.at[some], sem.at[0])
            self.came = pltpu.make_async_copy(dst.at[some], dst.at[some], sem.at[1])
            sent.append(self.left.wait)

        def start(self, pairs_of):
            for there, place, device in pairs_of:
                pltpu.make_async_remote_copy(
                    src_ref=self.src.at[there],
                    dst_ref=self.dst.at[place],
                    send_sem=self.sem.at[0],
                    recv_sem=self.sem.at[1],
                    device_id=device,
                    device_id_type=MESH,
                ).start()

        def wait_recv(self):
            self.came.wait()

    loads = [
        pltpu.make_async_copy(src, dst, in_sem.at[i])
        for i, (src, dst) in enumerate(
            [
                (enc_hbm, enc),
                (embed_hbm, embed),
                (wk_hbm, wqkv.at[0, 0:gw]),
                (wv_hbm, wqkv.at[0, gw : 2 * gw]),
                (wq_hbm, wqkv.at[0, 2 * gw : 3 * gw]),
                (pairs_hbm, pairs),
                (wo_hbm, wo.at[0]),
                (head_hbm, head.at[t]),
                (gain_q_hbm, gain_q),
                (gain_k_hbm, gain_k),
                (gain_o_hbm, gain_o),
            ]
        )
    ]
    barrier = pltpu.get_barrier_semaphore()
    far_first = [k for near in range(half, 0, -1) for k in sorted({near, nz - near})]
    reach = half // 2
    near = [k for k in far_first if min(k, nz - k) <= reach]
    far = [k for k in far_first if min(k, nz - k) > reach]
    partners = (
        [at_z_of(k) for k in near]
        + [at_d_of(lax.rem(d + r, nd)) for r in range(1, nd)]
        + [(img, lax.rem(t + r, tp)) for r in range(1, tp)]
    )
    for i, partner in enumerate(partners):
        if i == 5:
            for first in (5, 0, 1):
                loads[first].start()
        pl.semaphore_signal(barrier, inc=1, device_id=partner, device_id_type=MESH)

    lanes = pairs.shape[2]
    z_par = lanes // (nc * pairs_dev)
    blocks_y = nz // z_par
    log_img = imgs.bit_length() - 1
    log_c = nc.bit_length() - 1
    log_z = nz.bit_length() - 1

    def parts_of(ids):
        owner = ids >> log_img
        return ids & (imgs - 1), owner & (nc - 1), (owner >> log_c) & (nz - 1), owner >> (log_c + log_z)

    def lane_parts(shape):
        lane = iota(shape, 1)
        return lane // (nc * pairs_dev), (lane // pairs_dev) % nc, lane % pairs_dev

    loads[5].wait()
    taken = jnp.zeros((pairs.shape[0], lanes), F32)
    for side in range(2):
        im, oc, oz, oy = parts_of(pairs[:, side, :])
        taken = taken + jnp.where((oc == c) & (oz == z) & (oy == y), im + 1, 0).astype(F32)
    row, col = iota((slots, pairs.shape[0]), 0), iota((slots, pairs.shape[0]), 1)
    block_of = (row % nd) // nc * blocks_y + ((z + row // (tk * nd)) & (nz - 1)) // z_par
    spread = dot(one_hot(col == block_of).astype(BF16), taken.astype(BF16))
    row = iota((slots, lanes), 0)
    lane_par, lane_core, _ = lane_parts((slots, lanes))
    keep = (lane_par == ((z + row // (tk * nd)) & (z_par - 1))) & (lane_core == row % nc)
    which = jnp.sum(jnp.where(keep, spread, 0.0), axis=1, keepdims=True)
    row, col = iota((slots, tk * imgs), 0), iota((slots, tk * imgs), 1)
    slot_hot = one_hot((which == (col % imgs + 1).astype(F32)) & (col // imgs == (row // nd) % tk))
    slot_mat = slot_hot.astype(BF16)

    row, col = iota((tk * imgs, imgs * toks), 0), iota((tk * imgs, imgs * toks), 1)
    pick = one_hot(col == row % imgs * toks + t * tk + row // imgs).astype(BF16)
    loads[0].wait()
    mine = dot(pick, enc[...]).astype(BF16)
    loads[1].wait()
    for i in (2, 3, 4, 6, 7, 8, 9, 10):
        loads[i].start()

    def z_places(some):
        return [(k, nz - k, at_z_of(k)) for k in some]

    def send_z(src, dst, sem, h, now, later):
        return Swap(src[h], dst[h], sem.at[h], 0, z_places(now), more=later)

    def send_y(src, dst, sem, h):
        others = [lax.rem(d + r, nd) for r in sorted(range(1, nd), key=lambda r: abs(2 * r - nd))]
        return Swap(src[h], dst[h], sem.at[h], d, [(other, d, at_d_of(other)) for other in others])

    def send_x(src, dst, sem, h):
        others = [lax.rem(t + r, tp) for r in sorted(range(1, tp), key=lambda r: abs(2 * r - tp))]
        return Swap(src[h], dst[h], sem.at[h], t, [(other, t, (img, other)) for other in others])

    z_copies = []
    for h, start, width in going:
        embedded = dot(mine, embed[:, start : start + width]).astype(BF16)
        zs[h][...] = dot(slot_mat, embedded).astype(BF16).reshape(nz, tk * nd, width)
        if h == 0:
            pl.semaphore_wait(barrier, len(partners))
            for k in (reach, nz - reach):
                pl.semaphore_signal(far_sem, inc=1, device_id=at_z_of(k), device_id_type=MESH)
        z_copies.append(send_z(zs, zr, z_sem, h, near, far))
        if h == 0:
            pl.semaphore_wait(far_sem, 2)
        z_copies[h].start(z_places(far))

    next_t, prev_t = lax.rem(t + 1, tp), lax.rem(t + tp - 1, tp)
    far_t = lax.rem(t + 2, tp)
    sibling = (img + 1 - 2 * c, t)

    def weight_copies(which, buf, here, there_up, there_down, after, before, far_here, far_there):
        quarter = buf.shape[1] // 4

        def part(slot, first, count):
            start = (2 * c + first) * quarter
            return buf.at[slot, pl.ds(pl.multiple_of(start, quarter), count * quarter)]

        copies = {}

        def add(name, src, dst, device):
            i = len(copies)
            copies[name] = Send(src, dst, w_send.at[which, i], w_recv.at[which, i], device)

        add("up", part(here, 0, 2), part(there_up, 0, 2), (img, next_t))
        add("down", part(here, 0, 2), part(there_down, 0, 2), (img, prev_t))
        add("far_up", part(before, 0, 1), part(before if far_there is None else far_there, 0, 1), (img, next_t))
        add("far_down", part(after, 1, 1), part(after if far_there is None else far_there, 1, 1), (img, prev_t))
        add("before", part(before, 0, 2), part(before, 0, 2), sibling)
        add("after", part(after, 0, 2), part(after, 0, 2), sibling)
        add("far", part(far_here, 0, 2), part(far_here, 0, 2), sibling)
        return copies

    w_qkv = weight_copies(0, wqkv, 0, 3, 1, 1, 3, 2, 2)
    w_out = weight_copies(1, wo, 0, 3, 1, 1, 3, 2, 2)
    w_head = weight_copies(2, head, t, t, t, next_t, prev_t, far_t, None)

    def first_sends(w):
        w["up"].start()
        w["down"].start()

    def pass_on(w):
        w["up"].wait_recv()
        w["far_up"].start()
        w["down"].wait_recv()
        w["far_down"].start()
        w["before"].start()
        w["after"].start()

    def pass_far(w):
        w["far_up"].wait_recv()
        w["far_down"].wait_recv()
        w["far"].start()

    def arrive(w, name):
        w[name].wait_recv()

    for i in (2, 3, 4):
        loads[i].wait()
    first_sends(w_qkv)
    loads[6].wait()
    first_sends(w_out)

    row, col = iota((slots, slots), 0), iota((slots, slots), 1)
    same_token = (row // nz) % tk == (col // nd) % tk
    turn_mat = one_hot((row % nz == col // (tk * nd)) & (row // (tk * nz) == col % nd) & same_token).astype(BF16)
    same_token = (row // nd) % tk == (col // nz) % tk
    turn_back = one_hot((row // (tk * nd) == col % nz) & (row % nd == col // (tk * nz)) & same_token).astype(BF16)

    both = pairs[y * blocks_y + z // z_par]
    lane_par, lane_core, lane_pair = lane_parts((1, lanes))
    at_me = (lane_par == lax.rem(z, z_par)) & (lane_core == c)
    slot_rows = iota((nd * nz, lanes), 0)
    view = iota((views, lanes), 0)
    view_pair = view // (2 * pp) * pp + view % pp
    view_side = (view // pp) % 2
    view_mat = jnp.zeros((views, nd * nz), F32)
    back_mat = jnp.zeros((nd * nz, views), F32)
    for side in range(2):
        im, oc, oz, oy = parts_of(both[side : side + 1])
        code = jnp.where(at_me, (oy * nc + oc) * nz + ((oz - z + nz) & (nz - 1)), -1)
        from_hot = one_hot(slot_rows == code).astype(BF16)
        view_hot = one_hot(at_me & (lane_pair == view_pair) & (view_side == side)).astype(BF16)
        view_mat = view_mat + dot_t(view_hot, from_hot)
        back_mat = back_mat + dot_t(from_hot, view_hot)
    view_mat = view_mat.astype(BF16)
    back_mat = back_mat.astype(BF16)
    sum_mat = slot_hot.T.astype(BF16)

    y_copies = []
    for h, start, width in going:
        if h == len(going) - 1:
            pass_on(w_qkv)
            pass_on(w_out)
        z_copies[h].wait_recv()
        got = dot(turn_mat, zr[h][...].reshape(slots, width))
        ys[h][...] = got.astype(BF16).reshape(nd, tk, nz, width)
        y_copies.append(send_y(ys, yr, y_sem, h))
    pass_far(w_qkv)

    x_copies = []
    for h, start, width in going:
        y_copies[h].wait_recv()
        for ch in range(tk):
            got = dot(view_mat, yr[h][:, ch].reshape(nd * nz, width))
            xs[h][:, ch] = got.astype(BF16).reshape(tp, 2 * pp, width)
        x_copies.append(send_x(xs, xr, x_sem, h))

    pass_far(w_out)
    loads[7].wait()
    first_sends(w_head)
    for h in range(len(going)):
        x_copies[h].wait_recv()

    for i in (8, 9, 10):
        loads[i].wait()

    x = jnp.concatenate([xr[h][...].reshape(rows, width) for h, _, width in going], axis=1).astype(F32)
    base = norm_base(x)
    nq = (base * gain_q[...].astype(F32).reshape(1, dm)).astype(BF16)
    nk = (base * gain_k[...].astype(F32).reshape(1, dm)).astype(BF16)
    heads = gw // HEAD_DIM
    r0, r1 = iota((heads * rows, rows), 0) % rows, iota((heads * rows, rows), 1)
    seen = (r0 % pp == r1 % pp) & ((r0 // pp) % 2 != (r1 // pp) % 2)
    lane_head = iota((rows, gw), 1) // HEAD_DIM
    mixed = jnp.zeros((rows, dm), F32)
    for k, name in ((0, None), (3, "before"), (1, "after"), (2, "far")):
        if name:
            arrive(w_qkv, name)
        keys = dot_t(nk, wqkv[k, 0:gw]).astype(BF16)
        values = dot_t(nk, wqkv[k, gw : 2 * gw]).astype(BF16)
        query = (dot_t(nq, wqkv[k, 2 * gw : 3 * gw]) * HEAD_DIM ** (-0.5)).astype(BF16)
        each = [jnp.where(lane_head == h, query, jnp.zeros_like(query)) for h in range(heads)]
        scores = jnp.where(seen, dot_t(jnp.concatenate(each, axis=0), keys), -1e38)
        raised = jnp.exp(scores - jnp.max(scores, axis=-1, keepdims=True))
        weights = raised * (1.0 / jnp.sum(raised, axis=-1, keepdims=True))
        found = dot(weights.astype(BF16), values)
        attended = found[0:rows]
        for h in range(1, heads):
            attended = jnp.where(lane_head == h, found[h * rows : (h + 1) * rows], attended)
        if name:
            arrive(w_out, name)
        mixed = mixed + dot(attended.astype(BF16), wo[k]).astype(BF16).astype(F32)
    normed = norm_base(x + mixed) * gain_o[...].astype(F32).reshape(1, dm)
    for h, start, width in coming:
        ns[h][...] = normed[:, start : start + width].astype(BF16).reshape(tp, tk, 2 * pp, width)

    n_copies = [send_x(ns, nr, n_sem, h) for h in range(len(coming))]
    u_copies = []
    for h, start, width in coming:
        n_copies[h].wait_recv()
        for ch in range(tk):
            got = dot(back_mat, nr[h][:, ch].reshape(views, width))
            us[h][:, ch] = got.astype(BF16).reshape(nd, nz, width)
        u_copies.append(send_y(us, ur, u_sem, h))
    b_copies = []
    for h, start, width in coming:
        u_copies[h].wait_recv()
        got = dot(turn_back, ur[h][...].reshape(slots, width))
        bs[h][...] = got.astype(BF16).reshape(nz, tk * nd, width)
        b_copies.append(send_z(bs, br, b_sem, h, far_first, ()))

    pass_on(w_head)
    pass_far(w_head)
    for name in ("before", "after", "far"):
        arrive(w_head, name)

    maps = jnp.zeros((tk * imgs, tp * cols), F32)
    for h, start, width in coming:
        b_copies[h].wait_recv()
        summed = dot(sum_mat, br[h][...].reshape(slots, width)).astype(BF16)
        weight = head[...].reshape(dm, tp * cols)[start : start + width]
        maps = maps + dot(summed, weight)
    maps = maps.astype(BF16)
    for r in range(tp):
        oout[r] = maps[:, r * cols : (r + 1) * cols].reshape(tk, imgs, cols)
    others = [lax.rem(t + r, tp) for r in sorted(range(1, tp), key=lambda r: abs(2 * r - tp))]
    Swap(oout, out_ref, o_sem, t, [(other, t, (img, other)) for other in others], o_own).wait_recv()

    for wait in sent:
        wait()


def shards(
    encoded,
    pair_images,
    embed_w,
    gain_query,
    gain_key,
    gain_out,
    w_query,
    w_key,
    w_value,
    w_out,
    head_w,
):
    ny, nz, nc = GRID
    tp = lax.axis_size("tp")
    owners = lax.axis_size("img")
    imgs, toks, de = encoded.shape
    dm = embed_w.shape[1]
    gw = dm // tp
    tk = toks // tp
    pairs_dev = pair_images.shape[0] // owners
    pp = pairs_dev // tp
    cols = head_w.shape[1] // tp
    nd = ny * nc
    lanes = min(LANES, nz * nc * pairs_dev)
    blocks = pair_images.shape[0] // lanes
    pairs = pair_images.reshape(blocks, lanes, 2).transpose(0, 2, 1)
    dims = (ny, nz, nc, tp, imgs, toks, tk, pairs_dev, pp, dm, gw, cols)
    hbm = pl.BlockSpec(memory_space=pl.ANY)
    dma = pltpu.SemaphoreType.DMA
    def buffers(widths, *shape):
        return tuple(pltpu.VMEM((*shape, width), BF16) for width in widths)

    swap_z = nz, tk * nd
    swap_y = nd, tk, nz
    swap_x = tp, tk, 2 * pp
    out = pl.pallas_call(
        functools.partial(body, dims),
        name="sublayer",
        out_shape=jax.ShapeDtypeStruct((tp, tk, imgs, cols), BF16),
        in_specs=[hbm] * 11,
        out_specs=hbm,
        scratch_shapes=[
            pltpu.VMEM((dm,), BF16),
            pltpu.VMEM((dm,), BF16),
            pltpu.VMEM((dm,), BF16),
            pltpu.VMEM((imgs * toks, de), BF16),
            pltpu.VMEM(pairs.shape, jnp.int32),
            pltpu.VMEM(embed_w.shape, BF16),
            pltpu.VMEM((tp, 3 * gw, dm), BF16),
            pltpu.VMEM((tp, gw, dm), BF16),
            pltpu.VMEM((tp, gw, tp * cols), BF16),
            buffers(FORWARD, *swap_z),
            buffers(FORWARD, *swap_z),
            buffers(FORWARD, *swap_y),
            buffers(FORWARD, *swap_y),
            buffers(FORWARD, *swap_x),
            buffers(FORWARD, *swap_x),
            buffers(BACK, *swap_x),
            buffers(BACK, *swap_x),
            buffers(BACK, *swap_y),
            buffers(BACK, *swap_y),
            buffers(BACK, *swap_z),
            buffers(BACK, *swap_z),
            pltpu.VMEM((tp, tk, imgs, cols), BF16),
            dma((11,)),
            dma((len(FORWARD), 2)),
            dma((len(FORWARD), 2)),
            dma((len(FORWARD), 2)),
            dma((len(BACK), 2)),
            dma((len(BACK), 2)),
            dma((len(BACK), 2)),
            dma((2,)),
            dma,
            pltpu.SemaphoreType.REGULAR,
            dma((3, 7)),
            dma((3, 7)),
        ],
        compiler_params=pltpu.CompilerParams(
            collective_id=0, has_side_effects=True, vmem_limit_bytes=63 * 1024 * 1024
        ),
    )(
        encoded.reshape(imgs * toks, de),
        pairs,
        embed_w,
        gain_query,
        gain_key,
        gain_out,
        w_key.T,
        w_value.T,
        w_query.T,
        w_out,
        head_w,
    )
    return out.reshape(toks, imgs, cols).transpose(1, 0, 2)


def solution(mesh):
    placed = (
        P("img", None, None),
        P(),
        P(),
        P(),
        P(),
        P(),
        P(None, "tp"),
        P(None, "tp"),
        P(None, "tp"),
        P("tp", None),
        P("tp", None),
    )
    return jax.shard_map(
        shards, mesh=mesh, in_specs=placed, out_specs=P("img", None, "tp"), check_vma=False
    )
```

```python
import functools

import jax
import jax.numpy as jnp
from jax import lax
from jax.experimental import pallas as pl
from jax.experimental.pallas import tpu as pltpu
from jax.sharding import PartitionSpec as P

HEAD_DIM = 64
GRID = (4, 16, 2)
LANES = 128
FORWARD = (512, 256)
BACK = (256, 512)
MESH = pl.DeviceIdType.MESH
F32 = jnp.float32
BF16 = jnp.bfloat16


def iota(shape, dim):
    return lax.broadcasted_iota(jnp.int32, shape, dim)


def dot(a, b):
    return jnp.dot(a, b, preferred_element_type=F32)


def dot_t(a, b):
    return lax.dot_general(a, b, (((1,), (1,)), ((), ())), preferred_element_type=F32)


def one_hot(condition):
    return jnp.where(condition, 1.0, 0.0)


def norm_base(values):
    center = values - jnp.mean(values, axis=-1, keepdims=True)
    spread = jnp.mean(center * center, axis=-1, keepdims=True)
    return center * lax.rsqrt(spread + 1e-06)


def body(
    dims,
    enc_hbm,
    pairs_hbm,
    embed_hbm,
    gain_q_hbm,
    gain_k_hbm,
    gain_o_hbm,
    wk_hbm,
    wv_hbm,
    wq_hbm,
    wo_hbm,
    head_hbm,
    out_ref,
    gain_q,
    gain_k,
    gain_o,
    enc,
    pairs,
    embed,
    raw,
    wqkv,
    wo,
    head,
    zs,
    zr,
    ys,
    yr,
    xs,
    xr,
    ns,
    nr,
    us,
    ur,
    bs,
    br,
    oout,
    in_sem,
    z_sem,
    y_sem,
    x_sem,
    n_sem,
    u_sem,
    b_sem,
    o_sem,
    o_own,
    far_sem,
    w_send,
    w_recv,
):
    ny, nz, nc, tp, imgs, toks, tk, pairs_dev, pp, dm, gw, cols = dims
    nd = ny * nc
    half = nz // 2
    views = 2 * pairs_dev
    rows = tp * tk * 2 * pp
    going = [(h, sum(FORWARD[:h]), width) for h, width in enumerate(FORWARD)]
    coming = [(h, sum(BACK[:h]), width) for h, width in enumerate(BACK)]
    slots = nz * tk * nd
    img = lax.axis_index("img")
    t = lax.axis_index("tp")
    c = lax.rem(img, nc)
    z = lax.rem(lax.div(img, nc), nz)
    y = lax.div(img, nc * nz)
    d = y * nc + c
    line = img - z * nc
    plane = z * nc

    def at_z_of(k):
        return (line + lax.rem(z + k, nz) * nc, t)

    def at_d_of(other):
        return (plane + lax.div(other, nc) * (nz * nc) + lax.rem(other, nc), t)

    sent = []

    class Send:
        def __init__(self, src, dst, send, recv, device):
            self.copy = pltpu.make_async_remote_copy(
                src_ref=src, dst_ref=dst, send_sem=send, recv_sem=recv, device_id=device, device_id_type=MESH
            )

        def start(self):
            self.copy.start()
            sent.append(self.copy.wait_send)

        def wait_recv(self):
            self.copy.wait_recv()

    class Swap:
        def __init__(self, src, dst, sem, here, pairs_of, own=None, more=()):
            self.src, self.dst, self.sem = src, dst, sem
            self.start(pairs_of)
            if own is None:
                dst[here] = src[here]
            else:
                keep = pltpu.make_async_copy(src.at[here], dst.at[here], own)
                keep.start()
                sent.append(keep.wait)
            some = pl.ds(0, len(pairs_of) + len(more))
            self.left = pltpu.make_async_copy(src.at[some], src.at[some], sem.at[0])
            self.came = pltpu.make_async_copy(dst.at[some], dst.at[some], sem.at[1])
            sent.append(self.left.wait)

        def start(self, pairs_of):
            for there, place, device in pairs_of:
                pltpu.make_async_remote_copy(
                    src_ref=self.src.at[there],
                    dst_ref=self.dst.at[place],
                    send_sem=self.sem.at[0],
                    recv_sem=self.sem.at[1],
                    device_id=device,
                    device_id_type=MESH,
                ).start()

        def wait_recv(self):
            self.came.wait()

    loads = [
        pltpu.make_async_copy(src, dst, in_sem.at[i])
        for i, (src, dst) in enumerate(
            [
                (enc_hbm, enc),
                (embed_hbm, embed),
                (wk_hbm, raw.at[0:gw]),
                (wv_hbm, raw.at[gw : 2 * gw]),
                (wq_hbm, raw.at[2 * gw : 3 * gw]),
                (pairs_hbm, pairs),
                (wo_hbm, wo.at[0]),
                (head_hbm, head.at[t]),
                (gain_q_hbm, gain_q),
                (gain_k_hbm, gain_k),
                (gain_o_hbm, gain_o),
            ]
        )
    ]
    barrier = pltpu.get_barrier_semaphore()
    far_first = [k for near in range(half, 0, -1) for k in sorted({near, nz - near})]
    reach = half // 2
    near = [k for k in far_first if min(k, nz - k) <= reach]
    far = [k for k in far_first if min(k, nz - k) > reach]
    partners = (
        [at_z_of(k) for k in near]
        + [at_d_of(lax.rem(d + r, nd)) for r in range(1, nd)]
        + [(img, lax.rem(t + r, tp)) for r in range(1, tp)]
    )
    for i, partner in enumerate(partners):
        if i == 5:
            for first in (5, 0, 1, 2, 3, 4):
                loads[first].start()
        pl.semaphore_signal(barrier, inc=1, device_id=partner, device_id_type=MESH)

    lanes = pairs.shape[2]
    z_par = lanes // (nc * pairs_dev)
    blocks_y = nz // z_par
    log_img = imgs.bit_length() - 1
    log_c = nc.bit_length() - 1
    log_z = nz.bit_length() - 1

    def parts_of(ids):
        owner = ids >> log_img
        return ids & (imgs - 1), owner & (nc - 1), (owner >> log_c) & (nz - 1), owner >> (log_c + log_z)

    def lane_parts(shape):
        lane = iota(shape, 1)
        return lane // (nc * pairs_dev), (lane // pairs_dev) % nc, lane % pairs_dev

    loads[5].wait()
    taken = jnp.zeros((pairs.shape[0], lanes), F32)
    for side in range(2):
        im, oc, oz, oy = parts_of(pairs[:, side, :])
        taken = taken + jnp.where((oc == c) & (oz == z) & (oy == y), im + 1, 0).astype(F32)
    row, col = iota((slots, pairs.shape[0]), 0), iota((slots, pairs.shape[0]), 1)
    block_of = (row % nd) // nc * blocks_y + ((z + row // (tk * nd)) & (nz - 1)) // z_par
    spread = dot(one_hot(col == block_of).astype(BF16), taken.astype(BF16))
    row = iota((slots, lanes), 0)
    lane_par, lane_core, _ = lane_parts((slots, lanes))
    keep = (lane_par == ((z + row // (tk * nd)) & (z_par - 1))) & (lane_core == row % nc)
    which = jnp.sum(jnp.where(keep, spread, 0.0), axis=1, keepdims=True)
    row, col = iota((slots, tk * imgs), 0), iota((slots, tk * imgs), 1)
    slot_hot = one_hot((which == (col % imgs + 1).astype(F32)) & (col // imgs == (row // nd) % tk))
    slot_mat = slot_hot.astype(BF16)

    row, col = iota((tk * imgs, imgs * toks), 0), iota((tk * imgs, imgs * toks), 1)
    pick = one_hot(col == row % imgs * toks + t * tk + row // imgs).astype(BF16)
    loads[0].wait()
    mine = dot(pick, enc[...]).astype(BF16)
    loads[1].wait()
    for i in (6, 7, 8, 9, 10):
        loads[i].start()

    def z_places(some):
        return [(k, nz - k, at_z_of(k)) for k in some]

    def send_z(src, dst, sem, h, now, later):
        return Swap(src[h], dst[h], sem.at[h], 0, z_places(now), more=later)

    def send_y(src, dst, sem, h):
        others = [lax.rem(d + r, nd) for r in sorted(range(1, nd), key=lambda r: abs(2 * r - nd))]
        return Swap(src[h], dst[h], sem.at[h], d, [(other, d, at_d_of(other)) for other in others])

    def send_x(src, dst, sem, h):
        others = [lax.rem(t + r, tp) for r in sorted(range(1, tp), key=lambda r: abs(2 * r - tp))]
        return Swap(src[h], dst[h], sem.at[h], t, [(other, t, (img, other)) for other in others])

    next_t, prev_t = lax.rem(t + 1, tp), lax.rem(t + tp - 1, tp)
    far_t = lax.rem(t + 2, tp)
    sibling = (img + 1 - 2 * c, t)

    def weight_copies(which, buf, here, there_up, there_down, after, before, far_here, far_there):
        quarter = buf.shape[1] // 4

        def part(slot, first, count):
            start = (2 * c + first) * quarter
            return buf.at[slot, pl.ds(pl.multiple_of(start, quarter), count * quarter)]

        copies = {}

        def add(name, src, dst, device):
            i = len(copies)
            copies[name] = Send(src, dst, w_send.at[which, i], w_recv.at[which, i], device)

        add("up", part(here, 0, 2), part(there_up, 0, 2), (img, next_t))
        add("down", part(here, 0, 2), part(there_down, 0, 2), (img, prev_t))
        add("far_up", part(before, 0, 1), part(before if far_there is None else far_there, 0, 1), (img, next_t))
        add("far_down", part(after, 1, 1), part(after if far_there is None else far_there, 1, 1), (img, prev_t))
        add("before", part(before, 0, 2), part(before, 0, 2), sibling)
        add("after", part(after, 0, 2), part(after, 0, 2), sibling)
        add("far", part(far_here, 0, 2), part(far_here, 0, 2), sibling)
        return copies

    w_qkv = weight_copies(0, wqkv, 0, 3, 1, 1, 3, 2, 2)
    w_out = weight_copies(1, wo, 0, 3, 1, 1, 3, 2, 2)
    w_head = weight_copies(2, head, t, t, t, next_t, prev_t, far_t, None)

    def first_sends(w):
        w["up"].start()
        w["down"].start()

    def pass_on(w):
        w["up"].wait_recv()
        w["far_up"].start()
        w["down"].wait_recv()
        w["far_down"].start()
        w["before"].start()
        w["after"].start()

    def pass_far(w):
        w["far_up"].wait_recv()
        w["far_down"].wait_recv()
        w["far"].start()

    def arrive(w, name):
        w[name].wait_recv()

    raw[3 * gw :] = jnp.zeros((raw.shape[0] - 3 * gw, dm), BF16)
    for i in (2, 3, 4):
        loads[i].wait()
    wqkv[0] = raw[...].T
    z_copies = []
    for h, start, width in going:
        embedded = dot(mine, embed[:, start : start + width]).astype(BF16)
        zs[h][...] = dot(slot_mat, embedded).astype(BF16).reshape(nz, tk * nd, width)
        if h == 0:
            pl.semaphore_wait(barrier, len(partners))
            for k in (reach, nz - reach):
                pl.semaphore_signal(far_sem, inc=1, device_id=at_z_of(k), device_id_type=MESH)
            first_sends(w_qkv)
        z_copies.append(send_z(zs, zr, z_sem, h, near, far))
        if h == 0:
            pl.semaphore_wait(far_sem, 2)
        z_copies[h].start(z_places(far))

    loads[6].wait()
    first_sends(w_out)

    row, col = iota((slots, slots), 0), iota((slots, slots), 1)
    same_token = (row // nz) % tk == (col // nd) % tk
    turn_mat = one_hot((row % nz == col // (tk * nd)) & (row // (tk * nz) == col % nd) & same_token).astype(BF16)
    same_token = (row // nd) % tk == (col // nz) % tk
    turn_back = one_hot((row // (tk * nd) == col % nz) & (row % nd == col // (tk * nz)) & same_token).astype(BF16)

    both = pairs[y * blocks_y + z // z_par]
    lane_par, lane_core, lane_pair = lane_parts((1, lanes))
    at_me = (lane_par == lax.rem(z, z_par)) & (lane_core == c)
    slot_rows = iota((nd * nz, lanes), 0)
    view = iota((views, lanes), 0)
    view_pair = view // (2 * pp) * pp + view % pp
    view_side = (view // pp) % 2
    view_mat = jnp.zeros((views, nd * nz), F32)
    back_mat = jnp.zeros((nd * nz, views), F32)
    for side in range(2):
        im, oc, oz, oy = parts_of(both[side : side + 1])
        code = jnp.where(at_me, (oy * nc + oc) * nz + ((oz - z + nz) & (nz - 1)), -1)
        from_hot = one_hot(slot_rows == code).astype(BF16)
        view_hot = one_hot(at_me & (lane_pair == view_pair) & (view_side == side)).astype(BF16)
        view_mat = view_mat + dot_t(view_hot, from_hot)
        back_mat = back_mat + dot_t(from_hot, view_hot)
    view_mat = view_mat.astype(BF16)
    back_mat = back_mat.astype(BF16)
    sum_mat = slot_hot.T.astype(BF16)

    y_copies = []
    for h, start, width in going:
        if h == len(going) - 1:
            pass_on(w_qkv)
        z_copies[h].wait_recv()
        got = dot(turn_mat, zr[h][...].reshape(slots, width))
        ys[h][...] = got.astype(BF16).reshape(nd, tk, nz, width)
        y_copies.append(send_y(ys, yr, y_sem, h))
    pass_on(w_out)

    x_copies = []
    for h, start, width in going:
        y_copies[h].wait_recv()
        for ch in range(tk):
            got = dot(view_mat, yr[h][:, ch].reshape(nd * nz, width))
            xs[h][:, ch] = got.astype(BF16).reshape(tp, 2 * pp, width)
        x_copies.append(send_x(xs, xr, x_sem, h))

    pass_far(w_qkv)
    pass_far(w_out)
    loads[7].wait()
    first_sends(w_head)
    for h in range(len(going)):
        x_copies[h].wait_recv()

    for i in (8, 9, 10):
        loads[i].wait()

    x = jnp.concatenate([xr[h][...].reshape(rows, width) for h, _, width in going], axis=1).astype(F32)
    base = norm_base(x)
    nq = (base * gain_q[...].astype(F32).reshape(1, dm)).astype(BF16)
    nk = (base * gain_k[...].astype(F32).reshape(1, dm)).astype(BF16)
    heads = gw // HEAD_DIM
    r0, r1 = iota((heads * rows, rows), 0) % rows, iota((heads * rows, rows), 1)
    seen = (r0 % pp == r1 % pp) & ((r0 // pp) % 2 != (r1 // pp) % 2)
    lane_head = iota((rows, gw), 1) // HEAD_DIM
    order = ((0, None), (3, "before"), (1, "after"), (2, "far"))
    shares = []
    for k, name in order:
        if name:
            arrive(w_qkv, name)
        both = dot(nk, wqkv[k, :, 0 : 2 * gw]).astype(BF16)
        keys, values = both[:, 0:gw], both[:, gw:]
        query = (dot(nq, wqkv[k, :, 2 * gw :])[:, 0:gw] * HEAD_DIM ** (-0.5)).astype(BF16)
        shares.append((keys, values, query))
    for k, name in order[1:]:
        arrive(w_out, name)
    ones = jnp.ones((rows, gw), BF16)
    mixed = jnp.zeros((rows, dm), F32)
    for (k, _), (keys, values, query) in zip(order, shares):
        each = [jnp.where(lane_head == h, query, jnp.zeros_like(query)) for h in range(heads)]
        scores = jnp.where(seen, dot_t(jnp.concatenate(each, axis=0), keys), -1e38)
        raised = jnp.exp(scores - jnp.max(scores, axis=-1, keepdims=True)).astype(BF16)
        found, total = dot(raised, values), dot(raised, ones)
        attended, mass = found[0:rows], total[0:rows]
        for h in range(1, heads):
            attended = jnp.where(lane_head == h, found[h * rows : (h + 1) * rows], attended)
            mass = jnp.where(lane_head == h, total[h * rows : (h + 1) * rows], mass)
        attended = attended / mass
        mixed = mixed + dot(attended.astype(BF16), wo[k]).astype(BF16).astype(F32)
    normed = norm_base(x + mixed) * gain_o[...].astype(F32).reshape(1, dm)
    for h, start, width in coming:
        ns[h][...] = normed[:, start : start + width].astype(BF16).reshape(tp, tk, 2 * pp, width)

    n_copies = [send_x(ns, nr, n_sem, h) for h in range(len(coming))]
    u_copies = []
    for h, start, width in coming:
        n_copies[h].wait_recv()
        for ch in range(tk):
            got = dot(back_mat, nr[h][:, ch].reshape(views, width))
            us[h][:, ch] = got.astype(BF16).reshape(nd, nz, width)
        u_copies.append(send_y(us, ur, u_sem, h))
    b_copies = []
    for h, start, width in coming:
        u_copies[h].wait_recv()
        got = dot(turn_back, ur[h][...].reshape(slots, width))
        bs[h][...] = got.astype(BF16).reshape(nz, tk * nd, width)
        b_copies.append(send_z(bs, br, b_sem, h, far_first, ()))

    pass_on(w_head)
    pass_far(w_head)
    for name in ("before", "after", "far"):
        arrive(w_head, name)

    maps = jnp.zeros((tk * imgs, tp * cols), F32)
    for h, start, width in coming:
        b_copies[h].wait_recv()
        summed = dot(sum_mat, br[h][...].reshape(slots, width)).astype(BF16)
        weight = head[...].reshape(dm, tp * cols)[start : start + width]
        maps = maps + dot(summed, weight)
    maps = maps.astype(BF16)
    for r in range(tp):
        oout[r] = maps[:, r * cols : (r + 1) * cols].reshape(tk, imgs, cols)
    others = [lax.rem(t + r, tp) for r in sorted(range(1, tp), key=lambda r: abs(2 * r - tp))]
    earlier = len(sent)
    last = Swap(oout, out_ref, o_sem, t, [(other, t, (img, other)) for other in others], o_own)

    for wait in sent[:earlier]:
        wait()
    last.wait_recv()
    for wait in sent[earlier:]:
        wait()


def shards(
    encoded,
    pair_images,
    embed_w,
    gain_query,
    gain_key,
    gain_out,
    w_query,
    w_key,
    w_value,
    w_out,
    head_w,
):
    ny, nz, nc = GRID
    tp = lax.axis_size("tp")
    owners = lax.axis_size("img")
    imgs, toks, de = encoded.shape
    dm = embed_w.shape[1]
    gw = dm // tp
    tk = toks // tp
    pairs_dev = pair_images.shape[0] // owners
    pp = pairs_dev // tp
    cols = head_w.shape[1] // tp
    nd = ny * nc
    lanes = min(LANES, nz * nc * pairs_dev)
    blocks = pair_images.shape[0] // lanes
    pairs = pair_images.reshape(blocks, lanes, 2).transpose(0, 2, 1)
    dims = (ny, nz, nc, tp, imgs, toks, tk, pairs_dev, pp, dm, gw, cols)
    hbm = pl.BlockSpec(memory_space=pl.ANY)
    dma = pltpu.SemaphoreType.DMA
    def buffers(widths, *shape):
        return tuple(pltpu.VMEM((*shape, width), BF16) for width in widths)

    wide = -(-3 * gw // 128) * 128
    swap_z = nz, tk * nd
    swap_y = nd, tk, nz
    swap_x = tp, tk, 2 * pp
    out = pl.pallas_call(
        functools.partial(body, dims),
        name="sublayer",
        out_shape=jax.ShapeDtypeStruct((tp, tk, imgs, cols), BF16),
        in_specs=[hbm] * 11,
        out_specs=hbm,
        scratch_shapes=[
            pltpu.VMEM((dm,), BF16),
            pltpu.VMEM((dm,), BF16),
            pltpu.VMEM((dm,), BF16),
            pltpu.VMEM((imgs * toks, de), BF16),
            pltpu.VMEM(pairs.shape, jnp.int32),
            pltpu.VMEM(embed_w.shape, BF16),
            pltpu.VMEM((wide, dm), BF16),
            pltpu.VMEM((tp, dm, wide), BF16),
            pltpu.VMEM((tp, gw, dm), BF16),
            pltpu.VMEM((tp, gw, tp * cols), BF16),
            buffers(FORWARD, *swap_z),
            buffers(FORWARD, *swap_z),
            buffers(FORWARD, *swap_y),
            buffers(FORWARD, *swap_y),
            buffers(FORWARD, *swap_x),
            buffers(FORWARD, *swap_x),
            buffers(BACK, *swap_x),
            buffers(BACK, *swap_x),
            buffers(BACK, *swap_y),
            buffers(BACK, *swap_y),
            buffers(BACK, *swap_z),
            buffers(BACK, *swap_z),
            pltpu.VMEM((tp, tk, imgs, cols), BF16),
            dma((11,)),
            dma((len(FORWARD), 2)),
            dma((len(FORWARD), 2)),
            dma((len(FORWARD), 2)),
            dma((len(BACK), 2)),
            dma((len(BACK), 2)),
            dma((len(BACK), 2)),
            dma((2,)),
            dma,
            pltpu.SemaphoreType.REGULAR,
            dma((3, 7)),
            dma((3, 7)),
        ],
        compiler_params=pltpu.CompilerParams(
            collective_id=0, has_side_effects=True, vmem_limit_bytes=63 * 1024 * 1024
        ),
    )(
        encoded.reshape(imgs * toks, de),
        pairs,
        embed_w,
        gain_query,
        gain_key,
        gain_out,
        w_key.T,
        w_value.T,
        w_query.T,
        w_out,
        head_w,
    )
    return out.reshape(toks, imgs, cols).transpose(1, 0, 2)


def solution(mesh):
    placed = (
        P("img", None, None),
        P(),
        P(),
        P(),
        P(),
        P(),
        P(None, "tp"),
        P(None, "tp"),
        P(None, "tp"),
        P("tp", None),
        P("tp", None),
    )
    return jax.shard_map(
        shards, mesh=mesh, in_specs=placed, out_specs=P("img", None, "tp"), check_vma=False
    )
```

```python
import functools

import jax
import jax.numpy as jnp
from jax import lax
from jax.experimental import pallas as pl
from jax.experimental.pallas import tpu as pltpu
from jax.sharding import PartitionSpec as P

HEAD_DIM = 64
GRID = (4, 16, 2)
LANES = 128
FORWARD = (512, 256)
BACK = (256, 512)
MESH = pl.DeviceIdType.MESH
F32 = jnp.float32
BF16 = jnp.bfloat16


def iota(shape, dim):
    return lax.broadcasted_iota(jnp.int32, shape, dim)


def dot(a, b):
    return jnp.dot(a, b, preferred_element_type=F32)


def dot_t(a, b):
    return lax.dot_general(a, b, (((1,), (1,)), ((), ())), preferred_element_type=F32)


def one_hot(condition):
    return jnp.where(condition, 1.0, 0.0)


def norm_base(values):
    center = values - jnp.mean(values, axis=-1, keepdims=True)
    spread = jnp.mean(center * center, axis=-1, keepdims=True)
    return center * lax.rsqrt(spread + 1e-06)


def body(
    dims,
    enc_hbm,
    pairs_hbm,
    embed_hbm,
    gain_q_hbm,
    gain_k_hbm,
    gain_o_hbm,
    wk_hbm,
    wv_hbm,
    wq_hbm,
    wo_hbm,
    head_hbm,
    out_ref,
    gain_q,
    gain_k,
    gain_o,
    enc,
    pairs,
    embed,
    raw,
    wqkv,
    wo,
    head,
    zs,
    zr,
    ys,
    yr,
    xs,
    xr,
    ns,
    nr,
    us,
    ur,
    bs,
    br,
    oout,
    in_sem,
    z_sem,
    y_sem,
    x_sem,
    n_sem,
    u_sem,
    b_sem,
    o_sem,
    o_own,
    far_sem,
    w_send,
    w_recv,
):
    ny, nz, nc, tp, imgs, toks, tk, pairs_dev, pp, dm, gw, cols = dims
    nd = ny * nc
    half = nz // 2
    views = 2 * pairs_dev
    rows = tp * tk * 2 * pp
    going = [(h, sum(FORWARD[:h]), width) for h, width in enumerate(FORWARD)]
    coming = [(h, sum(BACK[:h]), width) for h, width in enumerate(BACK)]
    slots = nz * tk * nd
    img = lax.axis_index("img")
    t = lax.axis_index("tp")
    c = lax.rem(img, nc)
    z = lax.rem(lax.div(img, nc), nz)
    y = lax.div(img, nc * nz)
    d = y * nc + c
    line = img - z * nc
    plane = z * nc

    def at_z_of(k):
        return (line + lax.rem(z + k, nz) * nc, t)

    def at_d_of(other):
        return (plane + lax.div(other, nc) * (nz * nc) + lax.rem(other, nc), t)

    sent = []

    class Send:
        def __init__(self, src, dst, send, recv, device):
            self.copy = pltpu.make_async_remote_copy(
                src_ref=src, dst_ref=dst, send_sem=send, recv_sem=recv, device_id=device, device_id_type=MESH
            )

        def start(self):
            self.copy.start()
            sent.append(self.copy.wait_send)

        def wait_recv(self):
            self.copy.wait_recv()

    class Swap:
        def __init__(self, src, dst, sem, here, pairs_of, own=None, more=()):
            self.src, self.dst, self.sem = src, dst, sem
            self.start(pairs_of)
            if own is None:
                dst[here] = src[here]
            else:
                keep = pltpu.make_async_copy(src.at[here], dst.at[here], own)
                keep.start()
                sent.append(keep.wait)
            some = pl.ds(0, len(pairs_of) + len(more))
            self.left = pltpu.make_async_copy(src.at[some], src.at[some], sem.at[0])
            self.came = pltpu.make_async_copy(dst.at[some], dst.at[some], sem.at[1])
            sent.append(self.left.wait)

        def start(self, pairs_of):
            for there, place, device in pairs_of:
                pltpu.make_async_remote_copy(
                    src_ref=self.src.at[there],
                    dst_ref=self.dst.at[place],
                    send_sem=self.sem.at[0],
                    recv_sem=self.sem.at[1],
                    device_id=device,
                    device_id_type=MESH,
                ).start()

        def wait_recv(self):
            self.came.wait()

    loads = [
        pltpu.make_async_copy(src, dst, in_sem.at[i])
        for i, (src, dst) in enumerate(
            [
                (enc_hbm, enc),
                (embed_hbm, embed),
                (wk_hbm, raw.at[0:gw]),
                (wv_hbm, raw.at[gw : 2 * gw]),
                (wq_hbm, raw.at[2 * gw : 3 * gw]),
                (pairs_hbm, pairs),
                (wo_hbm, wo.at[0]),
                (head_hbm, head.at[t]),
                (gain_q_hbm, gain_q),
                (gain_k_hbm, gain_k),
                (gain_o_hbm, gain_o),
            ]
        )
    ]
    barrier = pltpu.get_barrier_semaphore()
    far_first = [k for near in range(half, 0, -1) for k in sorted({near, nz - near})]
    reach = half // 2
    near = [k for k in far_first if min(k, nz - k) <= reach]
    far = [k for k in far_first if min(k, nz - k) > reach]
    partners = (
        [at_z_of(k) for k in near]
        + [at_d_of(lax.rem(d + r, nd)) for r in range(1, nd)]
        + [(img, lax.rem(t + r, tp)) for r in range(1, tp)]
    )
    for i, partner in enumerate(partners):
        if i == 5:
            for first in (5, 0, 1, 2, 3, 4):
                loads[first].start()
        pl.semaphore_signal(barrier, inc=1, device_id=partner, device_id_type=MESH)

    lanes = pairs.shape[2]
    z_par = lanes // (nc * pairs_dev)
    blocks_y = nz // z_par
    log_img = imgs.bit_length() - 1
    log_c = nc.bit_length() - 1
    log_z = nz.bit_length() - 1

    def parts_of(ids):
        owner = ids >> log_img
        return ids & (imgs - 1), owner & (nc - 1), (owner >> log_c) & (nz - 1), owner >> (log_c + log_z)

    def lane_parts(shape):
        lane = iota(shape, 1)
        return lane // (nc * pairs_dev), (lane // pairs_dev) % nc, lane % pairs_dev

    loads[5].wait()
    taken = jnp.zeros((pairs.shape[0], lanes), F32)
    for side in range(2):
        im, oc, oz, oy = parts_of(pairs[:, side, :])
        taken = taken + jnp.where((oc == c) & (oz == z) & (oy == y), im + 1, 0).astype(F32)
    row, col = iota((slots, pairs.shape[0]), 0), iota((slots, pairs.shape[0]), 1)
    block_of = (row % nd) // nc * blocks_y + ((z + row // (tk * nd)) & (nz - 1)) // z_par
    spread = dot(one_hot(col == block_of).astype(BF16), taken.astype(BF16))
    row = iota((slots, lanes), 0)
    lane_par, lane_core, _ = lane_parts((slots, lanes))
    keep = (lane_par == ((z + row // (tk * nd)) & (z_par - 1))) & (lane_core == row % nc)
    which = jnp.sum(jnp.where(keep, spread, 0.0), axis=1, keepdims=True)
    row, col = iota((slots, tk * imgs), 0), iota((slots, tk * imgs), 1)
    slot_hot = one_hot((which == (col % imgs + 1).astype(F32)) & (col // imgs == (row // nd) % tk))
    slot_mat = slot_hot.astype(BF16)

    row, col = iota((tk * imgs, imgs * toks), 0), iota((tk * imgs, imgs * toks), 1)
    pick = one_hot(col == row % imgs * toks + t * tk + row // imgs).astype(BF16)
    loads[0].wait()
    mine = dot(pick, enc[...]).astype(BF16)
    loads[1].wait()
    for i in (6, 7, 8, 9, 10):
        loads[i].start()

    def z_places(some):
        return [(k, nz - k, at_z_of(k)) for k in some]

    def send_z(src, dst, sem, h, now, later):
        return Swap(src[h], dst[h], sem.at[h], 0, z_places(now), more=later)

    def send_y(src, dst, sem, h):
        others = [lax.rem(d + r, nd) for r in sorted(range(1, nd), key=lambda r: abs(2 * r - nd))]
        return Swap(src[h], dst[h], sem.at[h], d, [(other, d, at_d_of(other)) for other in others])

    def send_x(src, dst, sem, h):
        others = [lax.rem(t + r, tp) for r in sorted(range(1, tp), key=lambda r: abs(2 * r - tp))]
        return Swap(src[h], dst[h], sem.at[h], t, [(other, t, (img, other)) for other in others])

    next_t, prev_t = lax.rem(t + 1, tp), lax.rem(t + tp - 1, tp)
    far_t = lax.rem(t + 2, tp)
    sibling = (img + 1 - 2 * c, t)

    def weight_copies(which, buf, here, there_up, there_down, after, before, far_here, far_there):
        quarter = buf.shape[1] // 4

        def part(slot, first, count):
            start = (2 * c + first) * quarter
            return buf.at[slot, pl.ds(pl.multiple_of(start, quarter), count * quarter)]

        copies = {}

        def add(name, src, dst, device):
            i = len(copies)
            copies[name] = Send(src, dst, w_send.at[which, i], w_recv.at[which, i], device)

        add("up", part(here, 0, 2), part(there_up, 0, 2), (img, next_t))
        add("down", part(here, 0, 2), part(there_down, 0, 2), (img, prev_t))
        add("far_up", part(before, 0, 1), part(before if far_there is None else far_there, 0, 1), (img, next_t))
        add("far_down", part(after, 1, 1), part(after if far_there is None else far_there, 1, 1), (img, prev_t))
        add("before", part(before, 0, 2), part(before, 0, 2), sibling)
        add("after", part(after, 0, 2), part(after, 0, 2), sibling)
        add("far", part(far_here, 0, 2), part(far_here, 0, 2), sibling)
        return copies

    w_qkv = weight_copies(0, wqkv, 0, 3, 1, 1, 3, 2, 2)
    w_out = weight_copies(1, wo, 0, 3, 1, 1, 3, 2, 2)
    w_head = weight_copies(2, head, t, t, t, next_t, prev_t, far_t, None)

    def first_sends(w):
        w["up"].start()
        w["down"].start()

    def pass_on(w):
        w["up"].wait_recv()
        w["far_up"].start()
        w["down"].wait_recv()
        w["far_down"].start()
        w["before"].start()
        w["after"].start()

    def pass_far(w):
        w["far_up"].wait_recv()
        w["far_down"].wait_recv()
        w["far"].start()

    def arrive(w, name):
        w[name].wait_recv()

    raw[3 * gw :] = jnp.zeros((raw.shape[0] - 3 * gw, dm), BF16)
    for i in (2, 3, 4):
        loads[i].wait()
    wqkv[0] = raw[...].T
    z_copies = []
    for h, start, width in going:
        embedded = dot(mine, embed[:, start : start + width]).astype(BF16)
        zs[h][...] = dot(slot_mat, embedded).astype(BF16).reshape(nz, tk * nd, width)
        if h == 0:
            pl.semaphore_wait(barrier, len(partners))
            for k in (reach, nz - reach):
                pl.semaphore_signal(far_sem, inc=1, device_id=at_z_of(k), device_id_type=MESH)
            first_sends(w_qkv)
        z_copies.append(send_z(zs, zr, z_sem, h, near if h == 0 else far_first, far if h == 0 else ()))
        if h == 0:
            pl.semaphore_wait(far_sem, 2)
            z_copies[h].start(z_places(far))

    loads[6].wait()
    first_sends(w_out)

    row, col = iota((slots, slots), 0), iota((slots, slots), 1)
    same_token = (row // nz) % tk == (col // nd) % tk
    turn_mat = one_hot((row % nz == col // (tk * nd)) & (row // (tk * nz) == col % nd) & same_token).astype(BF16)
    same_token = (row // nd) % tk == (col // nz) % tk
    turn_back = one_hot((row // (tk * nd) == col % nz) & (row % nd == col // (tk * nz)) & same_token).astype(BF16)

    both = pairs[y * blocks_y + z // z_par]
    lane_par, lane_core, lane_pair = lane_parts((1, lanes))
    at_me = (lane_par == lax.rem(z, z_par)) & (lane_core == c)
    slot_rows = iota((nd * nz, lanes), 0)
    view = iota((views, lanes), 0)
    view_pair = view // (2 * pp) * pp + view % pp
    view_side = (view // pp) % 2
    view_mat = jnp.zeros((views, nd * nz), F32)
    back_mat = jnp.zeros((nd * nz, views), F32)
    for side in range(2):
        im, oc, oz, oy = parts_of(both[side : side + 1])
        code = jnp.where(at_me, (oy * nc + oc) * nz + ((oz - z + nz) & (nz - 1)), -1)
        from_hot = one_hot(slot_rows == code).astype(BF16)
        view_hot = one_hot(at_me & (lane_pair == view_pair) & (view_side == side)).astype(BF16)
        view_mat = view_mat + dot_t(view_hot, from_hot)
        back_mat = back_mat + dot_t(from_hot, view_hot)
    view_mat = view_mat.astype(BF16)
    back_mat = back_mat.astype(BF16)
    sum_mat = slot_hot.T.astype(BF16)

    y_copies = []
    for h, start, width in going:
        if h == len(going) - 1:
            pass_on(w_qkv)
        z_copies[h].wait_recv()
        got = dot(turn_mat, zr[h][...].reshape(slots, width))
        ys[h][...] = got.astype(BF16).reshape(nd, tk, nz, width)
        y_copies.append(send_y(ys, yr, y_sem, h))
    pass_on(w_out)

    x_copies = []
    for h, start, width in going:
        y_copies[h].wait_recv()
        for ch in range(tk):
            got = dot(view_mat, yr[h][:, ch].reshape(nd * nz, width))
            xs[h][:, ch] = got.astype(BF16).reshape(tp, 2 * pp, width)
        x_copies.append(send_x(xs, xr, x_sem, h))

    pass_far(w_qkv)
    pass_far(w_out)
    loads[7].wait()
    first_sends(w_head)
    for h in range(len(going)):
        x_copies[h].wait_recv()

    for i in (8, 9, 10):
        loads[i].wait()

    x = jnp.concatenate([xr[h][...].reshape(rows, width) for h, _, width in going], axis=1).astype(F32)
    base = norm_base(x)
    nq = (base * gain_q[...].astype(F32).reshape(1, dm)).astype(BF16)
    nk = (base * gain_k[...].astype(F32).reshape(1, dm)).astype(BF16)
    heads = gw // HEAD_DIM
    r0, r1 = iota((heads * rows, rows), 0) % rows, iota((heads * rows, rows), 1)
    seen = (r0 % pp == r1 % pp) & ((r0 // pp) % 2 != (r1 // pp) % 2)
    lane_head = iota((rows, gw), 1) // HEAD_DIM
    order = ((0, None), (3, "before"), (1, "after"), (2, "far"))
    shares = []
    for k, name in order:
        if name:
            arrive(w_qkv, name)
        both = dot(nk, wqkv[k, :, 0 : 2 * gw]).astype(BF16)
        keys, values = both[:, 0:gw], both[:, gw:]
        query = (dot(nq, wqkv[k, :, 2 * gw :])[:, 0:gw] * HEAD_DIM ** (-0.5)).astype(BF16)
        shares.append((keys, values, query))
    for k, name in order[1:]:
        arrive(w_out, name)
    ones = jnp.ones((rows, gw), BF16)
    mixed = jnp.zeros((rows, dm), F32)
    for (k, _), (keys, values, query) in zip(order, shares):
        each = [jnp.where(lane_head == h, query, jnp.zeros_like(query)) for h in range(heads)]
        scores = jnp.where(seen, dot_t(jnp.concatenate(each, axis=0), keys), -1e38)
        raised = jnp.exp(scores - jnp.max(scores, axis=-1, keepdims=True)).astype(BF16)
        found, total = dot(raised, values), dot(raised, ones)
        attended, mass = found[0:rows], total[0:rows]
        for h in range(1, heads):
            attended = jnp.where(lane_head == h, found[h * rows : (h + 1) * rows], attended)
            mass = jnp.where(lane_head == h, total[h * rows : (h + 1) * rows], mass)
        attended = attended / mass
        mixed = mixed + dot(attended.astype(BF16), wo[k]).astype(BF16).astype(F32)
    normed = norm_base(x + mixed) * gain_o[...].astype(F32).reshape(1, dm)
    for h, start, width in coming:
        ns[h][...] = normed[:, start : start + width].astype(BF16).reshape(tp, tk, 2 * pp, width)

    n_copies = [send_x(ns, nr, n_sem, h) for h in range(len(coming))]
    u_copies = []
    for h, start, width in coming:
        n_copies[h].wait_recv()
        for ch in range(tk):
            got = dot(back_mat, nr[h][:, ch].reshape(views, width))
            us[h][:, ch] = got.astype(BF16).reshape(nd, nz, width)
        u_copies.append(send_y(us, ur, u_sem, h))
    b_copies = []
    for h, start, width in coming:
        u_copies[h].wait_recv()
        got = dot(turn_back, ur[h][...].reshape(slots, width))
        bs[h][...] = got.astype(BF16).reshape(nz, tk * nd, width)
        b_copies.append(send_z(bs, br, b_sem, h, far_first, ()))

    pass_on(w_head)
    pass_far(w_head)
    for name in ("before", "after", "far"):
        arrive(w_head, name)

    maps = jnp.zeros((tk * imgs, tp * cols), F32)
    for h, start, width in coming:
        b_copies[h].wait_recv()
        summed = dot(sum_mat, br[h][...].reshape(slots, width)).astype(BF16)
        weight = head[...].reshape(dm, tp * cols)[start : start + width]
        maps = maps + dot(summed, weight)
    maps = maps.astype(BF16)
    for r in range(tp):
        oout[r] = maps[:, r * cols : (r + 1) * cols].reshape(tk, imgs, cols)
    others = [lax.rem(t + r, tp) for r in sorted(range(1, tp), key=lambda r: abs(2 * r - tp))]
    earlier = len(sent)
    last = Swap(oout, out_ref, o_sem, t, [(other, t, (img, other)) for other in others], o_own)

    for wait in sent[:earlier]:
        wait()
    last.wait_recv()
    for wait in sent[earlier:]:
        wait()


def shards(
    encoded,
    pair_images,
    embed_w,
    gain_query,
    gain_key,
    gain_out,
    w_query,
    w_key,
    w_value,
    w_out,
    head_w,
):
    ny, nz, nc = GRID
    tp = lax.axis_size("tp")
    owners = lax.axis_size("img")
    imgs, toks, de = encoded.shape
    dm = embed_w.shape[1]
    gw = dm // tp
    tk = toks // tp
    pairs_dev = pair_images.shape[0] // owners
    pp = pairs_dev // tp
    cols = head_w.shape[1] // tp
    nd = ny * nc
    lanes = min(LANES, nz * nc * pairs_dev)
    blocks = pair_images.shape[0] // lanes
    pairs = pair_images.reshape(blocks, lanes, 2).transpose(0, 2, 1)
    dims = (ny, nz, nc, tp, imgs, toks, tk, pairs_dev, pp, dm, gw, cols)
    hbm = pl.BlockSpec(memory_space=pl.ANY)
    dma = pltpu.SemaphoreType.DMA
    def buffers(widths, *shape):
        return tuple(pltpu.VMEM((*shape, width), BF16) for width in widths)

    wide = -(-3 * gw // 128) * 128
    swap_z = nz, tk * nd
    swap_y = nd, tk, nz
    swap_x = tp, tk, 2 * pp
    out = pl.pallas_call(
        functools.partial(body, dims),
        name="sublayer",
        out_shape=jax.ShapeDtypeStruct((tp, tk, imgs, cols), BF16),
        in_specs=[hbm] * 11,
        out_specs=hbm,
        scratch_shapes=[
            pltpu.VMEM((dm,), BF16),
            pltpu.VMEM((dm,), BF16),
            pltpu.VMEM((dm,), BF16),
            pltpu.VMEM((imgs * toks, de), BF16),
            pltpu.VMEM(pairs.shape, jnp.int32),
            pltpu.VMEM(embed_w.shape, BF16),
            pltpu.VMEM((wide, dm), BF16),
            pltpu.VMEM((tp, dm, wide), BF16),
            pltpu.VMEM((tp, gw, dm), BF16),
            pltpu.VMEM((tp, gw, tp * cols), BF16),
            buffers(FORWARD, *swap_z),
            buffers(FORWARD, *swap_z),
            buffers(FORWARD, *swap_y),
            buffers(FORWARD, *swap_y),
            buffers(FORWARD, *swap_x),
            buffers(FORWARD, *swap_x),
            buffers(BACK, *swap_x),
            buffers(BACK, *swap_x),
            buffers(BACK, *swap_y),
            buffers(BACK, *swap_y),
            buffers(BACK, *swap_z),
            buffers(BACK, *swap_z),
            pltpu.VMEM((tp, tk, imgs, cols), BF16),
            dma((11,)),
            dma((len(FORWARD), 2)),
            dma((len(FORWARD), 2)),
            dma((len(FORWARD), 2)),
            dma((len(BACK), 2)),
            dma((len(BACK), 2)),
            dma((len(BACK), 2)),
            dma((2,)),
            dma,
            pltpu.SemaphoreType.REGULAR,
            dma((3, 7)),
            dma((3, 7)),
        ],
        compiler_params=pltpu.CompilerParams(
            collective_id=0, has_side_effects=True, vmem_limit_bytes=63 * 1024 * 1024
        ),
    )(
        encoded.reshape(imgs * toks, de),
        pairs,
        embed_w,
        gain_query,
        gain_key,
        gain_out,
        w_key.T,
        w_value.T,
        w_query.T,
        w_out,
        head_w,
    )
    return out.reshape(toks, imgs, cols).transpose(1, 0, 2)


def solution(mesh):
    placed = (
        P("img", None, None),
        P(),
        P(),
        P(),
        P(),
        P(),
        P(None, "tp"),
        P(None, "tp"),
        P(None, "tp"),
        P("tp", None),
        P("tp", None),
    )
    return jax.shard_map(
        shards, mesh=mesh, in_specs=placed, out_specs=P("img", None, "tp"), check_vma=False
    )
```
